32 devices in a mesh: fsdp: 4 (over y, x), seq: 8 (over z, core).
Axes of the slice: x: 2, y: 2, z: 4, core: 2. Of those that a mesh axis runs over, the one named last changes fastest.
Arguments:
- tokens: bfloat16 [2, 4, 256, 8, 768], P(None, 'fsdp', None, 'seq'), may hold values from -6 to 6
- image_tokens: int32 [2, 4, 2, 3], P(None, 'fsdp'), may hold values from 0 to 1029, as said below
- ln1_gain: bfloat16 [768], P('fsdp'), may hold values from 0.099609375 to 1.8984375
- ln1_bias: bfloat16 [768], P('fsdp'), may hold values from -1.75 to 1.75
- qkv_weight: bfloat16 [768, 2304], P('fsdp'), may hold values from -0.21875 to 0.21875
- query_bias: bfloat16 [768], P('fsdp'), may hold values from -3 to 3
- value_bias: bfloat16 [768], P('fsdp'), may hold values from -3 to 3
- out_weight: bfloat16 [768, 768], P('fsdp'), may hold values from -3.5 to 3.5
- out_bias: bfloat16 [768], P('fsdp'), may hold values from -1.75 to 1.75
- scale_attn: bfloat16 [768], P('fsdp'), may hold values from 0.099609375 to 1.8984375
- ln2_gain: bfloat16 [768], P('fsdp'), may hold values from 0.099609375 to 1.8984375
- ln2_bias: bfloat16 [768], P('fsdp'), may hold values from -1.75 to 1.75
- up_weight: bfloat16 [768, 3072], P('fsdp'), may hold values from -0.21875 to 0.21875
- up_bias: bfloat16 [3072], P('fsdp'), may hold values from -3 to 3
- down_weight: bfloat16 [3072, 768], P('fsdp'), may hold values from -0.109375 to 0.109375
- down_bias: bfloat16 [768], P('fsdp'), may hold values from -1.75 to 1.75
- scale_mlp: bfloat16 [768], P('fsdp'), may hold values from 0.099609375 to 1.8984375
- cotangent: bfloat16 [2, 4, 256, 8, 768], P(None, 'fsdp', None, 'seq'), may hold values from -6 to 6
Outputs:
- output: bfloat16 [2, 4, 256, 8, 768], P(None, 'fsdp', None, 'seq')
- input_grad: bfloat16 [2, 4, 256, 8, 768], P(None, 'fsdp', None, 'seq')
- ln1_gain_grad: float32 [768], P('fsdp')
- ln1_bias_grad: float32 [768], P('fsdp')
- qkv_weight_grad: float32 [768, 2304], P('fsdp')
- query_bias_grad: float32 [768], P('fsdp')
- value_bias_grad: float32 [768], P('fsdp')
- out_weight_grad: float32 [768, 768], P('fsdp')
- out_bias_grad: float32 [768], P('fsdp')
- scale_attn_grad: float32 [768], P('fsdp')
- ln2_gain_grad: float32 [768], P('fsdp')
- ln2_bias_grad: float32 [768], P('fsdp')
- up_weight_grad: float32 [768, 3072], P('fsdp')
- up_bias_grad: float32 [3072], P('fsdp')
- down_weight_grad: float32 [3072, 768], P('fsdp')
- down_bias_grad: float32 [768], P('fsdp')
- scale_mlp_grad: float32 [768], P('fsdp')
The draws below stay inside these ranges and needn't reach their ends.
Inputs may be any that keep to these rules, and one draw needn't show every extreme that they name: `image_tokens`: in every micro-batch and image group exactly one slot, drawn at random, holds one image of 1029 tokens and nothing else; each other slot holds 2 to 3 images of 261 tokens. A row's nonzero counts come first. So a slot has at most 1029 places, and one has exactly that.
All inputs are finite; a program needn't handle non-finite values.
Results may differ from the reference program's by a relative error of at most 0.014.
Values may be sent and summed in bfloat16 or wider, within the bound.
No kernel may reach another device: no remote copies, remote signals or barrier semaphores. Data moves between devices by JAX's collectives and lax.ppermute only.
A program may use at most 192 MiB of HBM per device.

```python
import jax
import jax.numpy as jnp
from jax import lax

D = 768
FF = 3072
HEADS = 12
HEAD_DIM = 64
MICRO = 2
SHORT = 261
LONG = 1029
TOK_DEV = 256
L_GROUP = 2048
SLOTS = 2
SLOT_ROWS = 1032
KMAX = 3
KMIN = 2
N_FSDP = 4
N_SEQ = 8


def draw_image_tokens(key, part):
    key = jax.random.fold_in(key, 17)
    key_short, key_hot = jax.random.split(key)
    short_count = jax.random.randint(key_short, (MICRO, N_FSDP, SLOTS), KMIN, KMAX + 1)
    hottest = jax.random.randint(key_hot, (MICRO, N_FSDP, 1), 0, SLOTS)
    places = jnp.arange(KMAX)
    shorts = jnp.where(places[None, None, None, :] < short_count[..., None], SHORT, 0)
    long_row = jnp.where(places == 0, LONG, 0)
    chosen = jnp.arange(SLOTS)[None, None, :] == hottest
    return jnp.where(chosen[..., None], long_row[None, None, None, :], shorts).astype(jnp.int32)


def block_levels(key, extent, pieces, least, top_value):
    level = 1.0
    for axis_at, shards_of in pieces:
        heights = jax.random.uniform(jax.random.fold_in(jax.random.fold_in(key, 6), axis_at), (shards_of,), jnp.float32, least / len(pieces), top_value / len(pieces))
        level = level * jnp.repeat(jnp.exp(heights), extent[axis_at] // shards_of).reshape((-1,) + (1,) * (len(extent) - 1 - axis_at))
    return level


def normal_values(stream_key, dims, width, bound, pieces=(), held_as=jnp.bfloat16):
    factor_of = block_levels(stream_key, dims, pieces, -0.22, 0.18) if pieces else 1.0
    entries = jax.random.normal(stream_key, dims, jnp.float32) * width * factor_of
    return jnp.minimum(jnp.maximum(entries, -bound), bound).astype(held_as)


def setup_inputs(seed: int = 0) -> dict:
    key_of = jax.random.split(jax.random.key(seed), 19)
    return {
        "tokens": normal_values(key_of[0], (MICRO, N_FSDP, TOK_DEV, N_SEQ, D), 1.0, 6.0, ((1, 4), (3, 8))),
        "image_tokens": draw_image_tokens(jax.random.fold_in(key_of[18], 71), 0),
        "ln1_gain": jnp.clip(1.0 + 0.18 * jax.random.normal(key_of[2], (D,), jnp.float32), 0.099609375, 1.8984375).astype(jnp.bfloat16),
        "ln1_bias": normal_values(key_of[3], (D,), 0.3, 1.75, ((0, 4),)),
        "qkv_weight": normal_values(key_of[4], (D, 3 * D), D ** -0.5, 0.21875, ((0, 4),)),
        "query_bias": normal_values(key_of[5], (D,), 0.5, 3.0, ((0, 4),)),
        "value_bias": normal_values(key_of[6], (D,), 0.5, 3.0, ((0, 4),)),
        "out_weight": normal_values(key_of[7], (D, D), (D // SHORT + 1) ** -0.5, 3.5, ((0, 4),)),
        "out_bias": normal_values(key_of[8], (D,), 0.3, 1.75, ((0, 4),)),
        "scale_attn": jnp.clip(1.0 + 0.18 * jax.random.normal(key_of[9], (D,), jnp.float32), 0.099609375, 1.8984375).astype(jnp.bfloat16),
        "ln2_gain": jnp.clip(1.0 + 0.18 * jax.random.normal(key_of[10], (D,), jnp.float32), 0.099609375, 1.8984375).astype(jnp.bfloat16),
        "ln2_bias": normal_values(key_of[11], (D,), 0.3, 1.75, ((0, 4),)),
        "up_weight": normal_values(key_of[12], (D, FF), D ** -0.5, 0.21875, ((0, 4),)),
        "up_bias": normal_values(key_of[13], (FF,), 0.5, 3.0, ((0, 4),)),
        "down_weight": normal_values(key_of[14], (FF, D), FF ** -0.5, 0.109375, ((0, 4),)),
        "down_bias": normal_values(key_of[15], (D,), 0.3, 1.75, ((0, 4),)),
        "scale_mlp": jnp.clip(1.0 + 0.18 * jax.random.normal(key_of[16], (D,), jnp.float32), 0.099609375, 1.8984375).astype(jnp.bfloat16),
        "cotangent": normal_values(key_of[17], (MICRO, N_FSDP, TOK_DEV, N_SEQ, D), 1.0, 6.0, ((1, 4), (3, 8))),
    }


@jax.custom_vjp
def low(v):
    return lax.optimization_barrier(v.astype(jnp.bfloat16)).astype(jnp.float32)

@jax.custom_vjp
def low_back(v):
    return v

def low_keep(v):
    return (low(v), None)

def low_pass(kept, grad):
    return (grad,)

def back_keep(v):
    return (v, None)

def back_low(kept, grad):
    return (low(grad),)
low.defvjp(low_keep, low_pass)
low_back.defvjp(back_keep, back_low)
EPSILON = 1e-06
MASK_VALUE = -1e+30

def norm_rows(values, gain, shift):
    center = values - lax.optimization_barrier(jnp.mean(values, axis=-1, keepdims=True))
    spread = lax.optimization_barrier(jnp.mean(center * center, axis=-1, keepdims=True))
    return center * lax.rsqrt(spread + EPSILON) * gain + shift

def product(left, right):
    return jnp.dot(left, right, precision=lax.Precision.HIGHEST)

def slot_tables(counts):
    slot_sizes = lax.optimization_barrier(jnp.sum(counts, axis=1)).astype(jnp.int32)
    slot_starts = (jnp.cumsum(slot_sizes) - slot_sizes).astype(jnp.int32)
    image_ends = jnp.cumsum(counts.reshape(-1)).astype(jnp.int32)
    return (slot_sizes, slot_starts, image_ends)

def image_of(positions, image_ends):
    return lax.optimization_barrier(jnp.sum((image_ends[None, :] <= positions[:, None]).astype(jnp.int32), axis=1)).astype(jnp.int32)

def attend_slot(queries, key_rows, value_rows, segment):
    scores = jnp.einsum('hqd,hkd->hqk', queries, key_rows, precision=lax.Precision.HIGHEST) * HEAD_DIM ** (-0.5)
    scores = low_back(scores)
    same_image = segment[:, None] == segment[None, :]
    scores = jnp.where(same_image[None], scores, MASK_VALUE)
    weights = jax.nn.softmax(scores, axis=-1)
    return jnp.einsum('hqk,hkd->hqd', low(weights), value_rows, precision=lax.Precision.HIGHEST)

def group_layer(inputs, counts, params):
    ln1_gain, ln1_bias, qkv_weight, query_bias, value_bias, out_weight, out_bias, scale_attn, ln2_gain, ln2_bias, up_weight, up_bias, down_weight, down_bias, scale_mlp = params
    normed = low(norm_rows(inputs, ln1_gain, ln1_bias))
    shifts = jnp.concatenate([query_bias, jnp.zeros_like(query_bias), value_bias])
    projected = low_back(low(product(normed, qkv_weight) + shifts))
    slot_sizes, slot_starts, image_ends = slot_tables(counts)
    offsets = jnp.arange(SLOT_ROWS, dtype=jnp.int32)

    def one_slot(slot_index):
        is_live = offsets < slot_sizes[slot_index]
        where_rows = jnp.minimum(slot_starts[slot_index] + offsets, L_GROUP - 1).astype(jnp.int32)
        segment = jnp.where(is_live, image_of(where_rows, image_ends), -1)
        picked = jnp.take(projected, where_rows, axis=0).reshape(SLOT_ROWS, 3, HEADS, HEAD_DIM)
        heads_first = jnp.transpose(picked, (1, 2, 0, 3))
        result = attend_slot(heads_first[0], heads_first[1], heads_first[2], segment)
        return jnp.transpose(result, (1, 0, 2)).reshape(SLOT_ROWS, D) * is_live[:, None].astype(jnp.float32)
    per_slot = lax.map(jax.checkpoint(one_slot), jnp.arange(SLOTS, dtype=jnp.int32))
    live_all = offsets[None, :] < slot_sizes[:, None]
    scatter_rows = jnp.where(live_all, slot_starts[:, None] + offsets[None, :], L_GROUP).astype(jnp.int32)
    attended = jnp.zeros((L_GROUP + 1, D), jnp.float32).at[scatter_rows.reshape(-1)].add(per_slot.reshape(-1, D))[:L_GROUP]
    attended = low_back(low(attended))
    branch = low_back(product(attended, out_weight) + out_bias)
    middle = inputs + scale_attn * branch
    normed_second = low(norm_rows(middle, ln2_gain, ln2_bias))
    hidden = low_back(product(normed_second, up_weight) + up_bias)
    active = low(jax.nn.gelu(hidden, approximate=False))
    branch_two = low_back(product(active, down_weight) + down_bias)
    return middle + scale_mlp * branch_two

def reference(tokens, image_tokens, ln1_gain, ln1_bias, qkv_weight, query_bias, value_bias, out_weight, out_bias, scale_attn, ln2_gain, ln2_bias, up_weight, up_bias, down_weight, down_bias, scale_mlp, cotangent):
    params = tuple((item.astype(jnp.float32) for item in (ln1_gain, ln1_bias, qkv_weight, query_bias, value_bias, out_weight, out_bias, scale_attn, ln2_gain, ln2_bias, up_weight, up_bias, down_weight, down_bias, scale_mlp)))
    inputs = tokens.astype(jnp.float32).reshape(MICRO * N_FSDP, L_GROUP, D)
    counts = image_tokens.reshape(MICRO * N_FSDP, SLOTS, KMAX).astype(jnp.int32)

    def forward(group_inputs, weights):

        def one_group(members):
            return group_layer(members[0], members[1], weights)
        return lax.map(jax.checkpoint(one_group), (group_inputs, counts))
    outputs, pullback = jax.vjp(forward, inputs, params)
    input_grad, grads = pullback(cotangent.astype(jnp.float32).reshape(outputs.shape))
    full_shape = tokens.shape
    return (outputs.reshape(full_shape).astype(jnp.bfloat16), input_grad.reshape(full_shape).astype(jnp.bfloat16), grads[0], grads[1], grads[2], grads[3], grads[4], grads[5], grads[6], grads[7], grads[8], grads[9], grads[10], grads[11], grads[12], grads[13], grads[14])
```

```python
from functools import partial
from math import pi, sqrt

import jax
import jax.numpy as jnp
from jax import lax
from jax.experimental import pallas as pl
from jax.experimental.pallas import tpu as pltpu
from jax.sharding import PartitionSpec as P

LONG = 1029
EPSILON = 1e-06
MASK_VALUE = -1e30
PAD_SEGMENT = 127
LANES = 128
HEAD_WIDTH = 64
MIB = 2**20
BOTH = ("fsdp", "seq")
F32 = jnp.float32
BF16 = jnp.bfloat16
VMEM = pl.BlockSpec()
SMEM = pl.BlockSpec(memory_space=pltpu.SMEM)
ANY = pl.BlockSpec(memory_space=pl.ANY)

LN1_GAIN, LN1_BIAS, QUERY_BIAS, VALUE_BIAS, OUT_BIAS = 0, 1, 2, 3, 4
SCALE_ATTN, LN2_GAIN, LN2_BIAS, DOWN_BIAS, SCALE_MLP, UP_ROW = 5, 6, 7, 8, 9, 10


def ceil_to(value, step):
    return (value + step - 1) // step * step


def move(value, flips):
    fsdp_count, seq_count = lax.axis_size("fsdp"), lax.axis_size("seq")
    pairs = []
    for f in range(fsdp_count):
        for s in range(seq_count):
            fsdp_flip, chip_flip, core_flip = flips[s % 2]
            there = (f ^ fsdp_flip) * seq_count + (s ^ (2 * chip_flip + core_flip))
            pairs.append((f * seq_count + s, there))
    return lax.ppermute(value, BOTH, pairs)


def to_core(value):
    return move(value, [(0, 0, 1)] * 2)


def to_chip(value, flip, other_flip=None):
    return move(value, [(0, flip, 0), (0, flip if other_flip is None else other_flip, 0)])


def to_fsdp(value, flips):
    return move(value, [(flip, 0, 0) for flip in flips])


def wide(value):
    return value.astype(F32)


def dot(left, right):
    return jnp.dot(left, right, preferred_element_type=F32)


def rows_of(left, right):
    return lax.dot_general(left, right, (((0,), (0,)), ((), ())), preferred_element_type=F32)


def cols_of(left, right):
    return lax.dot_general(left, right, (((1,), (1,)), ((), ())), preferred_element_type=F32)


def shape(dims, dtype=BF16):
    return jax.ShapeDtypeStruct(dims, dtype)


def call(kernel, operands, outs, scratch=(), after=(), limit=62, aliases=None):
    count = len(operands)

    def run(*refs):
        kernel(*refs[:count], *refs[count + len(after) :])

    return pl.pallas_call(
        run,
        in_specs=[spec for _, spec in operands] + [ANY] * len(after),
        out_specs=[ANY if aliases else VMEM] * len(outs),
        out_shape=list(outs),
        scratch_shapes=list(scratch),
        input_output_aliases=aliases or {},
        compiler_params=pltpu.CompilerParams(vmem_limit_bytes=limit * MIB),
    )(*[array for array, _ in operands], *after)


def hold(arrays, after):
    results = call(
        lambda *refs: None,
        [(item, ANY) for item in arrays],
        [shape(item.shape, item.dtype) for item in arrays],
        after=after,
        aliases={i: i for i in range(len(arrays))},
    )
    return list(results)


def cut_kernel(begin, source, out):
    out[...] = source[begin : begin + out.shape[0], :]


def cut_rows(value, begin, count, after=()):
    out = shape((count, value.shape[1]))
    return call(partial(cut_kernel, begin), [(value, VMEM)], [out], after=after)[0]


def add_kernel(*refs):
    total = wide(refs[0][...])
    for ref in refs[1:-1]:
        total = total + wide(ref[...])
    refs[-1][...] = total.astype(BF16)


def add(items, after=()):
    return call(add_kernel, [(item, VMEM) for item in items], [shape(items[0].shape)], after=after)[0]


def places_of(counts_ref, slots, images, chip, source, tok_count, seq_count):
    micro, slot = chip // slots, chip % slots
    total = jnp.int32(0)
    ends, sizes = [], []
    for j in range(slots):
        size = jnp.int32(0)
        for i in range(images):
            size = size + counts_ref[micro, 0, j, i]
            ends.append(total + size)
        sizes.append(size)
        total = total + size
    free = seq_count * tok_count - total
    start, room_end = jnp.int32(0), jnp.int32(0)
    picked = [jnp.int32(0)] * 4
    for j in range(slots):
        room = LONG - sizes[j]
        span = (
            start,
            start + sizes[j],
            total + jnp.minimum(room_end, free),
            total + jnp.minimum(room_end + room, free),
        )
        picked = [jnp.where(slot == j, a, b) for a, b in zip(span, picked)]
        start, room_end = start + sizes[j], room_end + room
    first, last, more, stop = [(a - source + seq_count - 1) // seq_count for a in picked]
    return micro, first, last - first, more, stop - more, total, ends


def local_rows_of(step, first, count, more, extra):
    local = jnp.where(step < count, first + step, more + step - count)
    return local, step < count + extra


def prepare_kernel(sizes, groups, small_count, counts_ref, values, *refs):
    slots, images, chips, capacity, tok_count, seq_count = sizes
    shards, refs = refs[: sum(groups)], refs[sum(groups) :]
    smalls, refs = refs[:small_count], refs[small_count:]
    parts, halves, rest = refs[:chips], refs[chips : chips + len(groups)], refs[chips + len(groups) :]
    seq_index = lax.axis_index("seq")
    chip, core = seq_index // 2, seq_index % 2
    for flip in range(chips):
        micro, first, count, more, extra, _, _ = places_of(
            counts_ref, slots, images, chip ^ flip, seq_index, tok_count, seq_count
        )
        step = lax.broadcasted_iota(jnp.int32, (capacity, tok_count), 0)
        held = lax.broadcasted_iota(jnp.int32, (capacity, tok_count), 1)
        local, valid = local_rows_of(step, first, count, more, extra)
        pick = jnp.where(valid & (local == held), 1.0, 0.0).astype(BF16)
        start = pl.multiple_of(micro * tok_count, tok_count)
        parts[flip][...] = dot(pick, values[pl.ds(start, tok_count), :]).astype(BF16)
    if smalls:
        first_half, inserted = rest
        half = (halves[0].shape[0] - EXTRA_ROWS) // 2
        inserted[...] = jnp.zeros_like(inserted)
        for i, small in enumerate(smalls):
            length = small.shape[0]
            inserted[i : i + 1, :length] = small[...].astype(F32).reshape(1, length)
        halves[0][half : half + EXTRA_ROWS, : inserted.shape[1]] = inserted[...].astype(BF16)
    at = 0
    for count, out in zip(groups, halves):
        half = shards[at].shape[0] // 2
        for i in range(2):
            start = pl.multiple_of((core ^ i) * half, 16)
            row = i * (out.shape[0] - half)
            col = 0
            for shard in shards[at : at + count]:
                out[row : row + half, col : col + shard.shape[1]] = shard[pl.ds(start, half), :]
                col += shard.shape[1]
        at += count
    if smalls:
        first_half[...] = halves[0][: first_half.shape[0], :]
    else:
        marks_kernel(sizes, counts_ref, *rest)


def collect_kernel(sizes, counts_ref, *refs):
    slots, images, chips, capacity, tok_count, seq_count = sizes
    parts, out = refs[:chips], refs[chips]
    seq_index = lax.axis_index("seq")
    micros = chips // slots
    sums = [None] * micros
    for flip in range(chips):
        micro, first, count, more, extra, _, _ = places_of(
            counts_ref, slots, images, seq_index // 2 ^ flip, seq_index, tok_count, seq_count
        )
        step = lax.broadcasted_iota(jnp.int32, (tok_count, capacity), 1)
        held = lax.broadcasted_iota(jnp.int32, (tok_count, capacity), 0)
        local, valid = local_rows_of(step, first, count, more, extra)
        pick = jnp.where(valid & (local == held), 1.0, 0.0).astype(BF16)
        found = dot(pick, parts[flip][...])
        for m in range(micros):
            term = jnp.where(micro == m, found, 0.0)
            sums[m] = term if sums[m] is None else sums[m] + term
    for m in range(micros):
        out[m * tok_count : (m + 1) * tok_count, :] = sums[m].astype(BF16)


def marks_kernel(sizes, counts_ref, q_marks, k_marks, live_ref):
    slots, images, chips, capacity, tok_count, seq_count = sizes
    rows = chips * capacity
    seq_index = lax.axis_index("seq")
    chip, core = seq_index // 2, seq_index % 2
    row = lax.broadcasted_iota(jnp.int32, (rows, LANES), 0)
    lane = lax.broadcasted_iota(jnp.int32, (rows, LANES), 1)
    for which in range(2):
        segment = jnp.full((rows, LANES), PAD_SEGMENT, jnp.int32)
        live = jnp.zeros((rows, LANES), jnp.int32)
        for flip in range(chips):
            source = 2 * (chip ^ flip) + (core ^ which)
            _, first, count, more, extra, total, ends = places_of(
                counts_ref, slots, images, chip, source, tok_count, seq_count
            )
            step = row - flip * capacity
            local, valid = local_rows_of(step, first, count, more, extra)
            valid = valid & (step >= 0) & (step < capacity)
            place = local * seq_count + source
            image = jnp.zeros((rows, LANES), jnp.int32)
            for end in ends:
                image = image + (end <= place).astype(jnp.int32)
            segment = jnp.where(valid, image, segment)
            live = jnp.where(valid & (place < total), 1, live)
        same = segment == lane
        k_marks[which * rows : (which + 1) * rows, :] = jnp.where(same, 0.0, MASK_VALUE).astype(
            BF16
        )
        if which == 0:
            q_marks[...] = jnp.where(same, 1.0, 0.0).astype(BF16)
            live_ref[...] = live.astype(F32)


def stage(out, own, pieces, first_col, extra, sems):
    rows, cols = own.shape
    half = rows // 2
    mine, core = lax.axis_index("fsdp"), lax.axis_index("seq") % 2
    copies = []

    def put(source, flip, at):
        start = pl.multiple_of((mine ^ flip) * rows + at, 16)
        copy = pltpu.make_async_copy(
            source, out.at[pl.ds(start, source.shape[0])], sems.at[len(copies)]
        )
        copy.start()
        copies.append(copy)

    here = slice(first_col, first_col + cols)
    put(own, 0, 0)
    for i in range(2):
        home = core ^ i
        near, far = pieces[i], pieces[2 + i]
        put(near.at[:half, here], 1 + home, home * half)
        put(near.at[half + extra :, here], 1 + home, (1 - home) * half)
        put(far.at[:half, here], 3, home * half)
    return copies


def wait_all(copies):
    for copy in copies:
        copy.wait()


STAGE_SEMS = pltpu.SemaphoreType.DMA((7,))
EXTRA_ROWS = 16


def norm_parts(values):
    center = values - jnp.mean(values, axis=-1, keepdims=True)
    rstd = lax.rsqrt(jnp.mean(center * center, axis=-1, keepdims=True) + EPSILON)
    return center * rstd, rstd


def norm_back(e, xhat, rstd):
    return rstd * (
        e
        - jnp.mean(e, axis=-1, keepdims=True)
        - xhat * jnp.mean(e * xhat, axis=-1, keepdims=True)
    )


def vector(ref, row):
    return ref[row : row + 1, :]


def project_kernel(chips, *refs):
    x_parts, sent, own, pieces = refs[:chips], refs[chips], refs[chips + 1], refs[chips + 2 : chips + 6]
    x_rows, normed, q, k, v, vec, up_shift, weight, vectors, sems, vector_sems = refs[chips + 6 :]
    copies = stage(weight, own, pieces, 0, EXTRA_ROWS, sems)
    capacity, width = x_parts[0].shape
    half = own.shape[0] // 2
    mine, core = lax.axis_index("fsdp"), lax.axis_index("seq") % 2
    vector_copies = []
    for i, (source, flip) in enumerate(
        ((sent, 0), (pieces[0], 1 + core), (pieces[1], 2 - core), (pieces[2], 3))
    ):
        copy = pltpu.make_async_copy(
            source.at[half : half + EXTRA_ROWS, :width], vectors.at[mine ^ flip], vector_sems.at[i]
        )
        copy.start()
        vector_copies.append(copy)
    wait_all(vector_copies)
    shard = width // 4
    for f in range(4):
        row = lax.broadcasted_iota(jnp.int32, (shard, width), 0)
        col = lax.broadcasted_iota(jnp.int32, (shard, width), 1)
        shift = jnp.where(col == row + f * shard, 1.0, 0.0).astype(BF16)
        placed = dot(vectors[f, :, :shard], shift)
        vec[...] = placed if f == 0 else vec[...] + placed
        up_shift[:, f * width : (f + 1) * width] = vectors[f, UP_ROW : UP_ROW + 1, :].astype(F32)
    for i, part in enumerate(x_parts):
        here = slice(i * capacity, (i + 1) * capacity)
        x_rows[here, :] = part[...]
        xhat, _ = norm_parts(part[...].astype(F32))
        normed[here, :] = (xhat * vector(vec, LN1_GAIN) + vector(vec, LN1_BIAS)).astype(BF16)
    wait_all(copies)
    q[...] = (dot(normed[...], weight[:, :width]) + vector(vec, QUERY_BIAS)).astype(BF16)
    k[...] = dot(normed[...], weight[:, width : 2 * width]).astype(BF16)
    v[...] = (dot(normed[...], weight[:, 2 * width :]) + vector(vec, VALUE_BIAS)).astype(BF16)


def half_lanes(dims, which):
    lane = lax.broadcasted_iota(jnp.int32, dims, len(dims) - 1)
    return (lane < HEAD_WIDTH) == (which == 0)


def attend_forward_kernel(
    tiles, q_ref, own_k, own_v, other_k, other_v, qa_ref, ka_ref, live_ref, o_ref, lse_ref
):
    pair = pl.program_id(0)
    rows = q_ref.shape[0]
    row_tile = rows // tiles
    keys = jnp.concatenate([own_k[...], other_k[...]], axis=0)
    keys = jnp.concatenate([keys, ka_ref[...]], axis=1)
    values = jnp.concatenate([own_v[...], other_v[...]], axis=0)
    lane = lax.broadcasted_iota(jnp.int32, (row_tile, LANES), 1)
    for start in range(0, rows, row_tile):
        here = pl.ds(start, row_tile)
        scaled = q_ref[here, :] * jnp.asarray(HEAD_WIDTH**-0.5, BF16)
        marks = qa_ref[here, :]
        halves, lses = [], []
        for which in range(2):
            own = jnp.where(half_lanes(scaled.shape, which), scaled, jnp.zeros_like(scaled))
            scores = cols_of(jnp.concatenate([own, marks], axis=1), keys)
            peak = jnp.max(scores, axis=1, keepdims=True)
            weights = jnp.exp(scores - peak)
            total = jnp.sum(weights, axis=1, keepdims=True)
            halves.append(dot(weights.astype(BF16), values) / total)
            lses.append(peak + jnp.log(total))
        mixed = jnp.where(lane < HEAD_WIDTH, halves[0], halves[1])
        o_ref[here, :] = (mixed * live_ref[here, :]).astype(BF16)
        kept = jnp.where(pair == 0, jnp.zeros((row_tile, LANES), F32), lse_ref[here, :])
        kept = jnp.where(lane == 2 * pair, lses[0], kept)
        lse_ref[here, :] = jnp.where(lane == 2 * pair + 1, lses[1], kept)


def attention_specs(rows, first):
    per_pair = pl.BlockSpec((rows, LANES), lambda i: (0, i + first))
    two = pl.BlockSpec((2, rows, LANES), lambda i: (0, 0, i + first))
    whole = lambda n: pl.BlockSpec((n, LANES), lambda i: (0, 0))
    return per_pair, two, whole(rows), whole(2 * rows)


def ignoring(kernel, start, count):
    return lambda *refs: kernel(*refs[:start], *refs[start + count :])


def attend_forward(first, pairs_here, q, own_k, own_v, other_k, other_v, q_marks, k_marks, live, after=()):
    rows = q.shape[0]
    per_pair, _, marks, all_marks = attention_specs(rows, first)
    out_pair = attention_specs(rows, 0)[0]
    return pl.pallas_call(
        ignoring(partial(attend_forward_kernel, 4), 8, len(after)),
        grid=(pairs_here,),
        in_specs=[per_pair] * 5 + [marks, all_marks, marks] + [ANY] * len(after),
        out_specs=[out_pair, marks],
        out_shape=[shape((rows, pairs_here * LANES)), shape((rows, LANES), F32)],
        compiler_params=pltpu.CompilerParams(vmem_limit_bytes=62 * MIB),
    )(q, own_k, own_v, other_k, other_v, q_marks, k_marks, live, *after)


def widen_kernel(count, tile, *refs):
    attended_parts, refs = refs[:count], refs[count:]
    x_rows, vec, up_shift, own_out, own_up = refs[:5]
    pieces = refs[5:9]
    attended, branch, middle, normed, active, slope, out_weight, up_weight, out_sems, up_sems = refs[9:]
    out_cols = own_out.shape[1]
    out_copies = stage(out_weight, own_out, pieces, 0, 0, out_sems)
    up_copies = stage(up_weight, own_up, pieces, out_cols, 0, up_sems)
    at = 0
    for part in attended_parts:
        attended[:, at : at + part.shape[1]] = part[...]
        at += part.shape[1]
    wait_all(out_copies)
    rows, width = attended.shape
    for start in range(0, rows, tile):
        here = slice(start, start + tile)
        found = dot(attended[here, :], out_weight[...]) + vector(vec, OUT_BIAS)
        branch[here, :] = found
        mid = x_rows[here, :].astype(F32) + vector(vec, SCALE_ATTN) * found
        middle[here, :] = mid
        xhat, _ = norm_parts(mid)
        normed[here, :] = (xhat * vector(vec, LN2_GAIN) + vector(vec, LN2_BIAS)).astype(BF16)
    wait_all(up_copies)

    def widen(block, _):
        cols = pl.ds(pl.multiple_of(block * width, width), width)
        for start in range(0, rows, tile):
            here = slice(start, start + tile)
            hidden = dot(normed[here, :], up_weight[:, cols]) + up_shift[:, cols]
            bell = jnp.exp(-0.5 * hidden * hidden) * (1 / sqrt(2 * pi))
            below = 0.5 + 0.5 * lax.erf(hidden * sqrt(0.5))
            active[here, cols] = (hidden * below).astype(BF16)
            slope[here, cols] = (below + hidden * bell).astype(BF16)
        return 0

    lax.fori_loop(0, up_weight.shape[1] // width, widen, 0)


def down_kernel(chips, tile, *refs):
    active, slope, middle, vec, own = refs[:5]
    pieces, cots, refs = refs[5:9], refs[9 : 9 + chips], refs[9 + chips :]
    outs, refs = refs[:chips], refs[chips:]
    hidden_grad, sums, up_shift_grad = refs[:3]
    terms = refs[3:7]
    cot_rows, down_in, weight, sems = refs[7:]
    copies = stage(weight, own, pieces, 0, 0, sems)
    rows, width = middle.shape
    capacity = cots[0].shape[0]
    bias_sum = None
    for i, part in enumerate(cots):
        here = slice(i * capacity, (i + 1) * capacity)
        cot_rows[here, :] = part[...]
        scaled = (part[...].astype(F32) * vector(vec, SCALE_MLP)).astype(BF16)
        down_in[here, :] = scaled
        term = jnp.sum(scaled.astype(F32), axis=0, keepdims=True)
        bias_sum = term if i == 0 else bias_sum + term
    emit_terms(active, down_in, None, terms, 0)
    wait_all(copies)
    scale_sum = None
    for i in range(chips):
        here = slice(i * capacity, (i + 1) * capacity)
        found = dot(active[here, :], weight[...]) + vector(vec, DOWN_BIAS)
        outs[i][...] = (middle[here, :] + vector(vec, SCALE_MLP) * found).astype(BF16)
        term = jnp.sum(cot_rows[here, :].astype(F32) * found, axis=0, keepdims=True)
        scale_sum = term if i == 0 else scale_sum + term
    sums[0:1, :] = scale_sum
    sums[1:2, :] = bias_sum

    def back(block, _):
        cols = pl.ds(pl.multiple_of(block * width, width), width)
        total = None
        for start in range(0, rows, tile):
            here = slice(start, start + tile)
            grad = cols_of(down_in[here, :], weight[cols, :])
            grad = (grad * slope[here, cols].astype(F32)).astype(BF16)
            hidden_grad[here, cols] = grad
            term = jnp.sum(grad.astype(F32), axis=0, keepdims=True)
            total = term if start == 0 else total + term
        up_shift_grad[:, cols] = total
        return 0

    lax.fori_loop(0, hidden_grad.shape[1] // width, back, 0)


def narrow_kernel(chips, tile, *refs):
    hidden_grad, middle, branch, vec, own_out, own_up = refs[:6]
    pieces, cots, refs = refs[6:10], refs[10 : 10 + chips], refs[10 + chips :]
    middle_grad, branch_grad, attended_grad, sums = refs[:4]
    cot_rows, out_weight, up_weight, out_sems, up_sems = refs[4:]
    out_cols = own_out.shape[1]
    up_copies = stage(up_weight, own_up, pieces, out_cols, 0, up_sems)
    out_copies = stage(out_weight, own_out, pieces, 0, 0, out_sems)
    capacity = cots[0].shape[0]
    for i, part in enumerate(cots):
        cot_rows[i * capacity : (i + 1) * capacity, :] = part[...]
    wait_all(up_copies)
    rows = middle.shape[0]
    totals = [None] * 4
    for start in range(0, rows, tile):
        here = slice(start, start + tile)
        grad = cols_of(hidden_grad[here, :], up_weight[...])
        xhat, rstd = norm_parts(middle[here, :])
        mid = cot_rows[here, :].astype(F32) + norm_back(grad * vector(vec, LN2_GAIN), xhat, rstd)
        middle_grad[here, :] = mid
        back = (mid * vector(vec, SCALE_ATTN)).astype(BF16)
        branch_grad[here, :] = back
        for i, term in enumerate((grad * xhat, grad, mid * branch[here, :], back.astype(F32))):
            term = jnp.sum(term, axis=0, keepdims=True)
            totals[i] = term if start == 0 else totals[i] + term
    for i, total in enumerate(totals):
        sums[i : i + 1, :] = total
    wait_all(out_copies)
    for start in range(0, rows, tile):
        here = slice(start, start + tile)
        attended_grad[here, :] = cols_of(branch_grad[here, :], out_weight[...]).astype(BF16)


def up_terms_kernel(hidden_grad, normed, branch_grad, attended, *refs):
    terms, (up_scratch, out_scratch) = refs[:4], refs[4:]
    emit_terms(normed, hidden_grad, up_scratch, terms, 0)
    emit_terms(attended, branch_grad, out_scratch, terms, hidden_grad.shape[1])


def attend_backward_kernel(
    tiles,
    skipped,
    q_ref,
    own_k,
    own_v,
    other_k,
    other_v,
    qa_ref,
    ka_ref,
    live_ref,
    o_ref,
    lse_ref,
    g_ref,
    dq_ref,
    own_grad_ref,
    other_grad_ref,
    dk_sum,
    dv_sum,
):
    pair = pl.program_id(0) + skipped
    rows = q_ref.shape[0]
    row_tile = rows // tiles
    key_rows = jnp.concatenate([own_k[...], other_k[...]], axis=0)
    keys = jnp.concatenate([key_rows, ka_ref[...]], axis=1)
    values = jnp.concatenate([own_v[...], other_v[...]], axis=0)
    lane = lax.broadcasted_iota(jnp.int32, (row_tile, LANES), 1)
    scale = HEAD_WIDTH**-0.5
    for start in range(0, rows, row_tile):
        here = pl.ds(start, row_tile)
        scaled = q_ref[here, :] * jnp.asarray(scale, BF16)
        marks = qa_ref[here, :]
        grads = (g_ref[here, :] * live_ref[here, :]).astype(BF16)
        both = grads.astype(F32) * o_ref[here, :].astype(F32)
        halves = []
        key_part = value_part = None
        for which in range(2):
            mine = half_lanes(scaled.shape, which)
            own = jnp.where(mine, scaled, jnp.zeros_like(scaled))
            own_grads = jnp.where(mine, grads, jnp.zeros_like(grads))
            row_dot = jnp.sum(jnp.where(mine, both, 0.0), axis=1, keepdims=True)
            lse = jnp.sum(
                jnp.where(lane == 2 * pair + which, lse_ref[here, :], 0.0), axis=1, keepdims=True
            )
            scores = cols_of(jnp.concatenate([own, marks], axis=1), keys)
            probs = jnp.exp(scores - lse)
            prob_grads = cols_of(own_grads, values)
            score_grads = (probs * (prob_grads - row_dot)).astype(BF16)
            halves.append(dot(score_grads, key_rows))
            value_term = rows_of(probs.astype(BF16), own_grads)
            key_term = rows_of(score_grads, own)
            value_part = value_term if which == 0 else value_part + value_term
            key_part = key_term if which == 0 else key_part + key_term
        mixed = jnp.where(lane < HEAD_WIDTH, halves[0], halves[1])
        dq_ref[here, :] = (mixed * scale).astype(BF16)
        if start == 0:
            dk_sum[...] = key_part
            dv_sum[...] = value_part
        else:
            dk_sum[...] += key_part
            dv_sum[...] += value_part
    own_grad_ref[0] = dk_sum[:rows, :].astype(BF16)
    own_grad_ref[1] = dv_sum[:rows, :].astype(BF16)
    other_grad_ref[0] = dk_sum[rows:, :].astype(BF16)
    other_grad_ref[1] = dv_sum[rows:, :].astype(BF16)


def attend_backward(
    first, pairs_here, skipped, q, own_k, own_v, other_k, other_v, q_marks, k_marks, live, attended, lse, grads, after=()
):
    rows = q.shape[0]
    per_pair, _, marks, all_marks = attention_specs(rows, first)
    out_pair, out_two = attention_specs(rows, 0)[:2]
    there = attention_specs(rows, skipped)[0]
    return pl.pallas_call(
        ignoring(partial(attend_backward_kernel, 4, skipped), 11, len(after)),
        grid=(pairs_here,),
        in_specs=[per_pair] * 5 + [marks, all_marks, marks, there, marks, per_pair]
        + [ANY] * len(after),
        out_specs=[out_pair, out_two, out_two],
        out_shape=[shape((rows, pairs_here * LANES))]
        + [shape((2, rows, pairs_here * LANES))] * 2,
        scratch_shapes=[pltpu.VMEM((2 * rows, LANES), F32)] * 2,
        compiler_params=pltpu.CompilerParams(vmem_limit_bytes=62 * MIB),
    )(q, own_k, own_v, other_k, other_v, q_marks, k_marks, live, attended, lse, grads, *after)


def emit_terms(left, right, scratch, terms, at):
    away, keep, keep_far, keep_own = terms
    mine, core = lax.axis_index("fsdp"), lax.axis_index("seq") % 2
    count, cols = left.shape[1] // 4, right.shape[1]
    half = count // 2
    here = slice(at, at + cols)
    if scratch is not None:
        scratch[...] = rows_of(left[...], right[...])

    def rows_at(flip, which):
        start = (mine ^ flip) * count + which * half
        if scratch is not None:
            value = scratch[pl.ds(pl.multiple_of(start, 16), half), :]
        else:
            value = rows_of(left[:, pl.ds(pl.multiple_of(start, LANES), half)], right[...])
        return value.astype(BF16)

    for i in range(2):
        home = core ^ i
        rows = [rows_at(1 + home, home), rows_at(1 + home, 1 - home), rows_at(3, home), rows_at(0, home)]
        if i == 0:
            keep[:half, here] = rows[0]
            keep[half:, here] = rows[1]
            keep_far[:, here] = rows[2]
            keep_own[:, here] = rows[3]
        else:
            for j, value in enumerate(rows):
                away[j * half : (j + 1) * half, here] = value


def term_shapes(rows, cols):
    return [shape((count, cols)) for count in (2 * rows, rows, rows // 2, rows // 2)]


def far_kernel(keep_far, other, out):
    half = out.shape[0]
    out[...] = (wide(keep_far[...]) + wide(other[2 * half : 3 * half, :])).astype(BF16)


def near_kernel(keep, other, far, out):
    half = far.shape[0]
    first = wide(keep[:half, :]) + wide(other[:half, :]) + wide(far[...])
    out[:half, :] = first.astype(BF16)
    second = wide(keep[half:, :]) + wide(other[half : 2 * half, :])
    out[half:, :] = second.astype(BF16)


def half_kernel(keep_own, other, near, both, out):
    half = out.shape[0]
    total = wide(keep_own[...]) + wide(other[3 * half :, :]) + wide(near[:half, :])
    out[...] = (total + wide(both[...])).astype(BF16)


class Reduction:
    def __init__(self, terms):
        away, self.keep, self.keep_far, self.keep_own = terms
        self.half = shape(self.keep_far.shape)
        self.other = to_core(away)

    def send_far(self, after=()):
        operands = [(self.keep_far, VMEM), (self.other, VMEM)]
        self.far_sent = call(far_kernel, operands, [self.half], after=after)[0]
        self.far = to_fsdp(self.far_sent, (2, 1))

    def send_near(self, after=()):
        operands = [(self.keep, VMEM), (self.other, VMEM), (self.far, VMEM)]
        self.near_sent = call(near_kernel, operands, [shape(self.keep.shape)], after=after)[0]
        self.near = to_fsdp(self.near_sent, (1, 2))

    def send_both(self, after=()):
        count = self.half.shape[0]
        self.both_sent = cut_rows(self.near, count, count, after)
        self.both = to_core(self.both_sent)

    def send_chips(self, after=()):
        flips = [1 << i for i in range((lax.axis_size("seq") // 2).bit_length() - 1)]
        self.orders = list(zip(flips, flips[::-1]))
        operands = [(item, VMEM) for item in (self.keep_own, self.other, self.near, self.both)]
        self.sent = call(half_kernel, operands, [self.half], after=after)[0]
        self.got = to_chip(self.sent, *self.orders[0])

    def send_chips_again(self, after=()):
        for order in self.orders[1:]:
            self.sent = add([self.sent, self.got], after)
            self.got = to_chip(self.sent, *order)

    def send_total(self, after=()):
        self.total = add([self.sent, self.got], after)
        self.other_total = to_core(self.total)

    def shards(self, widths, after=()):
        outs = [shape((2 * self.half.shape[0], cols), F32) for cols in widths]
        operands = [(self.total, VMEM), (self.other_total, VMEM)]
        return call(spread_kernel, operands, outs, after=after)


def spread_kernel(own_ref, other_ref, *outs):
    core = lax.axis_index("seq") % 2
    half = own_ref.shape[0]
    at = 0
    for out in outs:
        cols = out.shape[1]
        for i, source in enumerate((own_ref, other_ref)):
            start = pl.multiple_of((core ^ i) * half, 16)
            out[pl.ds(start, half), :] = source[:, at : at + cols].astype(F32)
        at += cols


def project_grad_kernel(count, *refs):
    q_grads, own_grads, other_grads = refs[:count], refs[count : 2 * count], refs[2 * count : 3 * count]
    normed, projected_grad, sums = refs[3 * count : 3 * count + 3]
    terms, scratch = refs[3 * count + 3 : 3 * count + 7], refs[3 * count + 7]
    width = normed.shape[1]
    at = 0
    for q_grad, own_grad, other_grad in zip(q_grads, own_grads, other_grads):
        here = slice(at, at + q_grad.shape[1])
        projected_grad[:, here] = q_grad[...]
        sums[0:1, here] = jnp.sum(q_grad[...].astype(F32), axis=0, keepdims=True)
        for i in range(2):
            both = (own_grad[i].astype(F32) + other_grad[i].astype(F32)).astype(BF16)
            first = (i + 1) * width + at
            projected_grad[:, first : first + q_grad.shape[1]] = both
        sums[1:2, here] = jnp.sum(both.astype(F32), axis=0, keepdims=True)
        at += q_grad.shape[1]
    emit_terms(normed, projected_grad, scratch, terms, 0)


def input_kernel(chips, *refs):
    projected_grad, x_rows, middle_grad, vec, own = refs[:5]
    pieces, rest = refs[5:9], refs[9:]
    outs, sums, weight, sems = rest[:chips], rest[chips], rest[chips + 1], rest[chips + 2]
    copies = stage(weight, own, pieces, 0, EXTRA_ROWS, sems)
    capacity = outs[0].shape[0]
    wait_all(copies)
    totals = [None] * 2
    for i in range(chips):
        here = slice(i * capacity, (i + 1) * capacity)
        grad = cols_of(projected_grad[here, :], weight[...])
        xhat, rstd = norm_parts(x_rows[here, :].astype(F32))
        back = norm_back(grad * vector(vec, LN1_GAIN), xhat, rstd)
        outs[i][...] = (middle_grad[here, :] + back).astype(BF16)
        for j, term in enumerate((grad * xhat, grad)):
            term = jnp.sum(term, axis=0, keepdims=True)
            totals[j] = term if i == 0 else totals[j] + term
    sums[0:1, :] = totals[0]
    sums[1:2, :] = totals[1]


def body(
    tokens,
    image_tokens,
    ln1_gain,
    ln1_bias,
    qkv_weight,
    query_bias,
    value_bias,
    out_weight,
    out_bias,
    scale_attn,
    ln2_gain,
    ln2_bias,
    up_weight,
    up_bias,
    down_weight,
    down_bias,
    scale_mlp,
    cotangent,
):
    seq_count = lax.axis_size("seq")
    fsdp_index = lax.axis_index("fsdp")
    chips = seq_count // 2
    micro_count, tok_count, width = tokens.shape[0], tokens.shape[2], tokens.shape[4]
    slots, images = image_tokens.shape[2:]
    assert chips == micro_count * slots and lax.axis_size("fsdp") == 4
    assert slots * images < PAD_SEGMENT
    capacity = ceil_to((LONG - 2) // seq_count + 2, 16)
    rows = chips * capacity
    tile = rows // 2
    hidden_width = up_weight.shape[1]
    sizes = (slots, images, chips, capacity, tok_count, seq_count)
    counts = image_tokens

    def prepare(values, groups, small=(), after=(), send=True):
        flat = values.reshape(micro_count * tok_count, width)
        shards = [shard for group in groups for shard in group]
        more = EXTRA_ROWS if small else 0
        outs = [
            shape((group[0].shape[0] + more, sum(shard.shape[1] for shard in group)))
            for group in groups
        ]
        if small:
            outs += [shape((outs[0].shape[0] // 2 + more // 2, outs[0].shape[1]))]
        else:
            outs += [shape((rows, LANES)), shape((2 * rows, LANES)), shape((rows, LANES), F32)]
        results = call(
            partial(prepare_kernel, sizes, [len(group) for group in groups], len(small)),
            [(counts, SMEM)] + [(item, VMEM) for item in [flat] + shards + list(small)],
            [shape((capacity, width))] * chips + outs,
            [pltpu.VMEM((EXTRA_ROWS, width), F32)] if small else [],
            after=after,
        )
        parts = list(results[:chips])
        if send:
            for flip in range(chips - 1, 0, -1):
                parts[flip] = to_chip(parts[flip], flip)
        return parts, *results[chips:]

    def send(parts):
        return [parts[0]] + [to_chip(parts[flip], flip) for flip in range(1, chips)]

    def collect(parts, after=()):
        return call(
            partial(collect_kernel, sizes),
            [(counts, SMEM)] + [(part, VMEM) for part in parts],
            [shape((micro_count * tok_count, width))],
            after=after,
        )[0]

    small = [
        ln1_gain,
        ln1_bias,
        query_bias,
        value_bias,
        out_bias,
        scale_attn,
        ln2_gain,
        ln2_bias,
        down_bias,
        scale_mlp,
    ]
    own_rows = ln1_gain.shape[0]
    x_parts, qkv_sent, qkv_first = prepare(tokens, [[qkv_weight]], small + [up_bias])
    near, far = to_fsdp(qkv_sent, (1, 2)), to_fsdp(qkv_first, (3, 3))
    cot_sent, up_sent, down_sent, q_marks, k_marks, live = prepare(
        cotangent, [[out_weight, up_weight], [down_weight]], after=[qkv_sent], send=False
    )
    near, far, up_sent = hold([near, far, up_sent], x_parts + [q_marks])
    qkv_pieces = [near, to_core(near), far, to_core(far)]
    up_near = to_fsdp(up_sent, (1, 2))

    x_rows, normed_first, q, own_k, own_v, vec, up_shift = call(
        partial(project_kernel, chips),
        [(part, VMEM) for part in x_parts]
        + [(item, ANY) for item in [qkv_sent, qkv_weight] + qkv_pieces],
        [shape((rows, width))] * 5
        + [shape((EXTRA_ROWS, width), F32), shape((1, hidden_width), F32)],
        [
            pltpu.VMEM((width, 3 * width), BF16),
            pltpu.VMEM((4, EXTRA_ROWS, width), BF16),
            STAGE_SEMS,
            pltpu.SemaphoreType.DMA((4,)),
        ],
    )
    attention = (q, own_k, own_v, to_core(own_k), to_core(own_v), q_marks, k_marks, live)
    step = width // LANES // 3
    attended_parts, lses = [], []

    def forward(i, after=()):
        part, lse = attend_forward(i * step, step, *attention, after=attended_parts[-1:] + list(after))
        attended_parts.append(part)
        lses.append(lse)

    forward(0)
    up_near, down_sent, *cot_sent = hold([up_near, down_sent] + cot_sent, attended_parts[-1:])
    cot_parts = send(cot_sent)
    up_first = cut_rows(up_near, 0, own_rows // 2)
    up_far = to_fsdp(up_first, (2, 1))
    down_near = to_fsdp(down_sent, (1, 2))
    forward(1, [up_first])
    up_far, *cot_parts = hold([up_far] + cot_parts, attended_parts[-1:])
    up_pieces = [up_near, to_core(up_near), up_far, to_core(up_far)]
    forward(2, [up_far])
    down_near = hold([down_near], attended_parts[-1:])[0]
    down_first = cut_rows(down_near, 0, down_weight.shape[0] // 2)
    down_far = to_fsdp(down_first, (2, 1))

    up_scratch = [
        pltpu.VMEM((width, width), BF16),
        pltpu.VMEM((width, hidden_width), BF16),
        STAGE_SEMS,
        STAGE_SEMS,
    ]
    attended, branch, middle, normed_second, active, slope = call(
        partial(widen_kernel, len(attended_parts), tile),
        [(item, VMEM) for item in attended_parts + [x_rows, vec, up_shift]]
        + [(item, ANY) for item in [out_weight, up_weight] + up_pieces],
        [
            shape((rows, width)),
            shape((rows, width), F32),
            shape((rows, width), F32),
            shape((rows, width)),
            shape((rows, hidden_width)),
            shape((rows, hidden_width)),
        ],
        up_scratch,
        after=[down_first],
    )
    down_far = hold([down_far], [attended])[0]
    down_pieces = [down_near, to_core(down_near), down_far, to_core(down_far)]
    results = call(
        partial(down_kernel, chips, tile),
        [(item, VMEM) for item in (active, slope, middle, vec)]
        + [(item, ANY) for item in [down_weight] + down_pieces]
        + [(part, VMEM) for part in cot_parts],
        [shape((capacity, width))] * chips
        + [
            shape((rows, hidden_width)),
            shape((2, width), F32),
            shape((1, hidden_width), F32),
        ]
        + term_shapes(down_weight.shape[0], width),
        [
            pltpu.VMEM((rows, width), BF16),
            pltpu.VMEM((rows, width), BF16),
            pltpu.VMEM((hidden_width, width), BF16),
            STAGE_SEMS,
        ],
    )
    out_sent, results = results[:chips], results[chips:]
    hidden_grad, down_sums, up_shift_grad, *down_terms = results
    down = Reduction(down_terms)
    out_parts = send(out_sent)

    middle_grad, branch_grad, attended_grad, narrow_sums = call(
        partial(narrow_kernel, chips, tile),
        [(item, VMEM) for item in (hidden_grad, middle, branch, vec)]
        + [(item, ANY) for item in [out_weight, up_weight] + up_pieces]
        + [(part, VMEM) for part in cot_parts],
        [
            shape((rows, width), F32),
            shape((rows, width)),
            shape((rows, width)),
            shape((4, width), F32),
        ],
        [pltpu.VMEM((rows, width), BF16)] + up_scratch,
    )
    down.send_far([middle_grad])
    up_terms = call(
        up_terms_kernel,
        [(item, VMEM) for item in (hidden_grad, normed_second, branch_grad, attended)],
        term_shapes(own_rows, hidden_width + width),
        [pltpu.VMEM((width, hidden_width), F32), pltpu.VMEM((width, width), F32)],
        after=[down.far_sent],
    )
    up = Reduction(up_terms)
    down.send_near([up_terms[0]])

    query_grads, own_grads, other_grads = [], [], []

    def backward(first, count, after):
        query_grad, own_grad, other_grad = attend_backward(
            first,
            count,
            first % step,
            *attention,
            attended_parts[first // step],
            lses[first // step],
            attended_grad,
            after=after + query_grads[-1:],
        )
        query_grads.append(query_grad)
        own_grads.append(own_grad)
        other_grads.append(to_core(other_grad))

    backward(0, 1, [down.near_sent])
    up.send_far(query_grads[-1:])
    out_parts = hold(out_parts, query_grads[-1:])
    backward(1, 1, [up.far_sent, out_parts[-1]])
    down.send_both(query_grads[-1:])
    backward(2, 1, [down.both_sent])
    down.send_chips(query_grads[-1:])
    up.send_near(query_grads[-1:])
    backward(3, 1, [down.sent, up.near_sent])
    backward(4, 1, [])
    down.send_chips_again(query_grads[-1:])
    up.send_both(query_grads[-1:])
    backward(5, 1, [down.sent, up.both_sent])
    up.send_chips(query_grads[-1:])

    projected_grad, qkv_sums, *qkv_terms = call(
        partial(project_grad_kernel, len(query_grads)),
        [(item, VMEM) for item in query_grads + own_grads + other_grads + [normed_first]],
        [shape((rows, 3 * width)), shape((2, width), F32)] + term_shapes(own_rows, 3 * width),
        [pltpu.VMEM((width, 3 * width), F32)],
        after=[up.sent],
    )
    qkv = Reduction(qkv_terms)
    down.send_total([projected_grad])
    qkv.send_far([down.total])
    *in_sent, input_sums = call(
        partial(input_kernel, chips),
        [(item, VMEM) for item in (projected_grad, x_rows, middle_grad, vec)]
        + [(item, ANY) for item in [qkv_weight] + qkv_pieces],
        [shape((capacity, width))] * chips + [shape((2, width), F32)],
        [pltpu.VMEM((width, 3 * width), BF16), STAGE_SEMS],
        after=[qkv.far_sent],
    )
    up.send_chips_again([input_sums])
    qkv.send_near([input_sums])
    in_parts = send(in_sent)
    output = collect(out_parts, [qkv.near_sent])
    (down_grad,) = down.shards([width], [output])
    qkv.send_both([down_grad])
    qkv.send_chips()
    up.send_total()
    up_grad, out_grad = up.shards([hidden_width, width], [qkv.sent])
    qkv.send_chips_again([up_grad])
    input_grad = collect(in_parts, [qkv.sent])
    qkv.send_total([input_grad])
    (qkv_grad,) = qkv.shards([3 * width])
    output, input_grad = output.reshape(tokens.shape), input_grad.reshape(tokens.shape)

    vector_grads = jnp.concatenate(
        [
            input_sums,
            qkv_sums,
            narrow_sums[3:4],
            narrow_sums[2:3],
            narrow_sums[0:2],
            down_sums[1:2],
            down_sums[0:1],
        ]
    )
    vector_grads = jnp.transpose(vector_grads.reshape(10, 4, -1), (1, 0, 2))
    vector_grads = jnp.concatenate([vector_grads, up_shift_grad.reshape(4, 4, -1)], 1)
    vector_grads = vector_grads + to_core(vector_grads)
    for flip in (1, 2):
        vector_grads = vector_grads + to_fsdp(vector_grads, (flip, flip))
    step = 1
    while step < chips:
        vector_grads = vector_grads + to_chip(vector_grads, step)
        step *= 2
    small_grads = lax.dynamic_index_in_dim(vector_grads, fsdp_index, 0, keepdims=False)

    return (
        output,
        input_grad,
        small_grads[LN1_GAIN],
        small_grads[LN1_BIAS],
        qkv_grad,
        small_grads[QUERY_BIAS],
        small_grads[VALUE_BIAS],
        out_grad,
        small_grads[OUT_BIAS],
        small_grads[SCALE_ATTN],
        small_grads[LN2_GAIN],
        small_grads[LN2_BIAS],
        up_grad,
        small_grads[10:].reshape(-1),
        down_grad,
        small_grads[DOWN_BIAS],
        small_grads[SCALE_MLP],
    )


def solution(mesh):
    vector, matrix = P("fsdp"), P("fsdp", None)
    places = P(None, "fsdp", None, "seq", None)
    return jax.shard_map(
        body,
        mesh=mesh,
        in_specs=(
            places,
            P(None, "fsdp", None, None),
            vector,
            vector,
            matrix,
            vector,
            vector,
            matrix,
            vector,
            vector,
            vector,
            vector,
            matrix,
            vector,
            matrix,
            vector,
            vector,
            places,
        ),
        out_specs=(
            places,
            places,
            vector,
            vector,
            matrix,
            vector,
            vector,
            matrix,
            vector,
            vector,
            vector,
            vector,
            matrix,
            vector,
            matrix,
            vector,
            vector,
        ),
        check_vma=False,
    )
```

```python
from functools import partial
from math import pi, sqrt

import jax
import jax.numpy as jnp
from jax import lax
from jax.experimental import pallas as pl
from jax.experimental.pallas import tpu as pltpu
from jax.sharding import PartitionSpec as P

LONG = 1029
EPSILON = 1e-06
MASK_VALUE = -1e30
PAD_SEGMENT = 127
LANES = 128
HEAD_WIDTH = 64
MIB = 2**20
BOTH = ("fsdp", "seq")
F32 = jnp.float32
BF16 = jnp.bfloat16
VMEM = pl.BlockSpec()
SMEM = pl.BlockSpec(memory_space=pltpu.SMEM)
ANY = pl.BlockSpec(memory_space=pl.ANY)

LN1_GAIN, LN1_BIAS, QUERY_BIAS, VALUE_BIAS, OUT_BIAS = 0, 1, 2, 3, 4
SCALE_ATTN, LN2_GAIN, LN2_BIAS, DOWN_BIAS, SCALE_MLP, UP_ROW = 5, 6, 7, 8, 9, 10


def ceil_to(value, step):
    return (value + step - 1) // step * step


def move(value, flips):
    fsdp_count, seq_count = lax.axis_size("fsdp"), lax.axis_size("seq")
    pairs = []
    for f in range(fsdp_count):
        for s in range(seq_count):
            fsdp_flip, chip_flip, core_flip = flips[s % 2]
            there = (f ^ fsdp_flip) * seq_count + (s ^ (2 * chip_flip + core_flip))
            pairs.append((f * seq_count + s, there))
    return lax.ppermute(value, BOTH, pairs)


def to_core(value):
    return move(value, [(0, 0, 1)] * 2)


def to_chip(value, flip, other_flip=None):
    return move(value, [(0, flip, 0), (0, flip if other_flip is None else other_flip, 0)])


def to_fsdp(value, flips):
    return move(value, [(flip, 0, 0) for flip in flips])


def wide(value):
    return value.astype(F32)


def dot(left, right):
    return jnp.dot(left, right, preferred_element_type=F32)


def rows_of(left, right):
    return lax.dot_general(left, right, (((0,), (0,)), ((), ())), preferred_element_type=F32)


def cols_of(left, right):
    return lax.dot_general(left, right, (((1,), (1,)), ((), ())), preferred_element_type=F32)


def shape(dims, dtype=BF16):
    return jax.ShapeDtypeStruct(dims, dtype)


def call(kernel, operands, outs, scratch=(), after=(), limit=16, aliases=None):
    count = len(operands)

    def run(*refs):
        kernel(*refs[:count], *refs[count + len(after) :])

    return pl.pallas_call(
        run,
        in_specs=[spec for _, spec in operands] + [ANY] * len(after),
        out_specs=[ANY if aliases else VMEM] * len(outs),
        out_shape=list(outs),
        scratch_shapes=list(scratch),
        input_output_aliases=aliases or {},
        compiler_params=pltpu.CompilerParams(vmem_limit_bytes=limit * MIB),
    )(*[array for array, _ in operands], *after)


def hold(arrays, after):
    results = call(
        lambda *refs: None,
        [(item, ANY) for item in arrays],
        [shape(item.shape, item.dtype) for item in arrays],
        after=after,
        aliases={i: i for i in range(len(arrays))},
    )
    return list(results)


def flips_of(label, chips):
    bits = chips.bit_length() - 1
    return sum(((label >> i) & 1) << (bits - 1 - i) for i in range(bits)), label


def flip_of(label, core, chips):
    first, second = flips_of(label, chips)
    return label if first == second else jnp.where(core == 0, first, second)


def places_of(counts_ref, slots, images, chip, source, tok_count, seq_count):
    micro, slot = chip // slots, chip % slots
    total = jnp.int32(0)
    ends, sizes = [], []
    for j in range(slots):
        size = jnp.int32(0)
        for i in range(images):
            size = size + counts_ref[micro, 0, j, i]
            ends.append(total + size)
        sizes.append(size)
        total = total + size
    free = seq_count * tok_count - total
    start, room_end = jnp.int32(0), jnp.int32(0)
    picked = [jnp.int32(0)] * 4
    for j in range(slots):
        room = LONG - sizes[j]
        span = (
            start,
            start + sizes[j],
            total + jnp.minimum(room_end, free),
            total + jnp.minimum(room_end + room, free),
        )
        picked = [jnp.where(slot == j, a, b) for a, b in zip(span, picked)]
        start, room_end = start + sizes[j], room_end + room
    first, last, more, stop = [(a - source + seq_count - 1) // seq_count for a in picked]
    return micro, first, last - first, more, stop - more, total, ends


def local_rows_of(step, first, count, more, extra):
    local = jnp.where(step < count, first + step, more + step - count)
    return local, step < count + extra


def prepare_kernel(sizes, groups, small_count, counts_ref, values, *refs):
    slots, images, chips, capacity, tok_count, seq_count = sizes
    shards, refs = refs[: sum(groups)], refs[sum(groups) :]
    smalls, refs = refs[:small_count], refs[small_count:]
    parts, halves, rest = refs[:chips], refs[chips : chips + len(groups)], refs[chips + len(groups) :]
    seq_index = lax.axis_index("seq")
    chip, core = seq_index // 2, seq_index % 2
    for label in range(chips):
        flip = flip_of(label, core, chips)
        micro, first, count, more, extra, _, _ = places_of(
            counts_ref, slots, images, chip ^ flip, seq_index, tok_count, seq_count
        )
        step = lax.broadcasted_iota(jnp.int32, (capacity, tok_count), 0)
        held = lax.broadcasted_iota(jnp.int32, (capacity, tok_count), 1)
        local, valid = local_rows_of(step, first, count, more, extra)
        pick = jnp.where(valid & (local == held), 1.0, 0.0).astype(BF16)
        start = pl.multiple_of(micro * tok_count, tok_count)
        parts[label][...] = dot(pick, values[pl.ds(start, tok_count), :]).astype(BF16)
    if smalls:
        first_half, inserted = rest
        half = (halves[0].shape[0] - EXTRA_ROWS) // 2
        inserted[...] = jnp.zeros_like(inserted)
        for i, small in enumerate(smalls):
            length = small.shape[0]
            inserted[i : i + 1, :length] = small[...].astype(F32).reshape(1, length)
        halves[0][half : half + EXTRA_ROWS, : inserted.shape[1]] = inserted[...].astype(BF16)
    at = 0
    for count, out in zip(groups, halves):
        half = shards[at].shape[0] // 2
        for i in range(2):
            start = pl.multiple_of((core ^ i) * half, 16)
            row = i * (out.shape[0] - half)
            col = 0
            for shard in shards[at : at + count]:
                out[row : row + half, col : col + shard.shape[1]] = shard[pl.ds(start, half), :]
                col += shard.shape[1]
        at += count
    if smalls:
        first_half[...] = halves[0][: first_half.shape[0], :]
    else:
        marks_kernel(sizes, counts_ref, *rest)


def collect_kernel(sizes, counts_ref, *refs):
    slots, images, chips, capacity, tok_count, seq_count = sizes
    parts, out = refs[:chips], refs[chips]
    seq_index = lax.axis_index("seq")
    micros = chips // slots
    sums = [None] * micros
    for label in range(chips):
        flip = flip_of(label, seq_index % 2, chips)
        micro, first, count, more, extra, _, _ = places_of(
            counts_ref, slots, images, seq_index // 2 ^ flip, seq_index, tok_count, seq_count
        )
        step = lax.broadcasted_iota(jnp.int32, (tok_count, capacity), 1)
        held = lax.broadcasted_iota(jnp.int32, (tok_count, capacity), 0)
        local, valid = local_rows_of(step, first, count, more, extra)
        pick = jnp.where(valid & (local == held), 1.0, 0.0).astype(BF16)
        found = dot(pick, parts[label][...])
        for m in range(micros):
            term = jnp.where(micro == m, found, 0.0)
            sums[m] = term if sums[m] is None else sums[m] + term
    for m in range(micros):
        out[m * tok_count : (m + 1) * tok_count, :] = sums[m].astype(BF16)


def marks_kernel(sizes, counts_ref, q_marks, k_marks, live_ref):
    slots, images, chips, capacity, tok_count, seq_count = sizes
    rows = chips * capacity
    seq_index = lax.axis_index("seq")
    chip, core = seq_index // 2, seq_index % 2
    row = lax.broadcasted_iota(jnp.int32, (rows, LANES), 0)
    lane = lax.broadcasted_iota(jnp.int32, (rows, LANES), 1)
    for which in range(2):
        segment = jnp.full((rows, LANES), PAD_SEGMENT, jnp.int32)
        live = jnp.zeros((rows, LANES), jnp.int32)
        for label in range(chips):
            flip = flip_of(label, core ^ which, chips)
            source = 2 * (chip ^ flip) + (core ^ which)
            _, first, count, more, extra, total, ends = places_of(
                counts_ref, slots, images, chip, source, tok_count, seq_count
            )
            step = row - label * capacity
            local, valid = local_rows_of(step, first, count, more, extra)
            valid = valid & (step >= 0) & (step < capacity)
            place = local * seq_count + source
            image = jnp.zeros((rows, LANES), jnp.int32)
            for end in ends:
                image = image + (end <= place).astype(jnp.int32)
            segment = jnp.where(valid, image, segment)
            live = jnp.where(valid & (place < total), 1, live)
        same = segment == lane
        k_marks[which * rows : (which + 1) * rows, :] = jnp.where(same, 0.0, MASK_VALUE).astype(
            BF16
        )
        if which == 0:
            q_marks[...] = jnp.where(same, 1.0, 0.0).astype(BF16)
            live_ref[...] = live.astype(F32)


def stage(out, own, pieces, first_col, extra, sems):
    rows, cols = own.shape
    half = rows // 2
    mine, core = lax.axis_index("fsdp"), lax.axis_index("seq") % 2
    copies = []

    def put(source, flip, at):
        start = pl.multiple_of((mine ^ flip) * rows + at, 16)
        copy = pltpu.make_async_copy(
            source, out.at[pl.ds(start, source.shape[0])], sems.at[len(copies)]
        )
        copy.start()
        copies.append(copy)

    here = slice(first_col, first_col + cols)
    put(own, 0, 0)
    for i in range(2):
        home = core ^ i
        near, far = pieces[i], pieces[2 + i]
        put(near.at[:half, here], 1 + home, home * half)
        put(near.at[half + extra :, here], 1 + home, (1 - home) * half)
        put(far.at[:half, here], 3, home * half)
    return copies


def wait_all(copies):
    for copy in copies:
        copy.wait()


STAGE_SEMS = pltpu.SemaphoreType.DMA((7,))
EXTRA_ROWS = 16


def norm_parts(values):
    center = values - jnp.mean(values, axis=-1, keepdims=True)
    rstd = lax.rsqrt(jnp.mean(center * center, axis=-1, keepdims=True) + EPSILON)
    return center * rstd, rstd


def norm_back(e, xhat, rstd):
    return rstd * (
        e
        - jnp.mean(e, axis=-1, keepdims=True)
        - xhat * jnp.mean(e * xhat, axis=-1, keepdims=True)
    )


def vector(ref, row):
    return ref[row : row + 1, :]


def project_kernel(chips, *refs):
    x_parts, sent, own, pieces = refs[:chips], refs[chips], refs[chips + 1], refs[chips + 2 : chips + 6]
    x_rows, normed, q, k, v, vec, up_shift, weight, vectors, sems, vector_sems = refs[chips + 6 :]
    copies = stage(weight, own, pieces, 0, EXTRA_ROWS, sems)
    capacity, width = x_parts[0].shape
    half = own.shape[0] // 2
    mine, core = lax.axis_index("fsdp"), lax.axis_index("seq") % 2
    vector_copies = []
    for i, (source, flip) in enumerate(
        ((sent, 0), (pieces[0], 1 + core), (pieces[1], 2 - core), (pieces[2], 3))
    ):
        copy = pltpu.make_async_copy(
            source.at[half : half + EXTRA_ROWS, :width], vectors.at[mine ^ flip], vector_sems.at[i]
        )
        copy.start()
        vector_copies.append(copy)
    wait_all(vector_copies)
    shard = width // 4
    for f in range(4):
        row = lax.broadcasted_iota(jnp.int32, (shard, width), 0)
        col = lax.broadcasted_iota(jnp.int32, (shard, width), 1)
        shift = jnp.where(col == row + f * shard, 1.0, 0.0).astype(BF16)
        placed = dot(vectors[f, :, :shard], shift)
        vec[...] = placed if f == 0 else vec[...] + placed
        up_shift[:, f * width : (f + 1) * width] = vectors[f, UP_ROW : UP_ROW + 1, :].astype(F32)
    for i, part in enumerate(x_parts):
        here = slice(i * capacity, (i + 1) * capacity)
        x_rows[here, :] = part[...]
        xhat, _ = norm_parts(part[...].astype(F32))
        normed[here, :] = (xhat * vector(vec, LN1_GAIN) + vector(vec, LN1_BIAS)).astype(BF16)
    wait_all(copies)
    q[...] = (dot(normed[...], weight[:, :width]) + vector(vec, QUERY_BIAS)).astype(BF16)
    k[...] = dot(normed[...], weight[:, width : 2 * width]).astype(BF16)
    v[...] = (dot(normed[...], weight[:, 2 * width :]) + vector(vec, VALUE_BIAS)).astype(BF16)


def half_lanes(dims, which):
    lane = lax.broadcasted_iota(jnp.int32, dims, len(dims) - 1)
    return (lane < HEAD_WIDTH) == (which == 0)


def attend_forward_kernel(
    tiles, q_ref, own_k, own_v, other_k, other_v, qa_ref, ka_ref, live_ref, o_ref, lse_ref
):
    pair = pl.program_id(0)
    rows = q_ref.shape[0]
    row_tile = rows // tiles
    keys = jnp.concatenate([own_k[...], other_k[...]], axis=0)
    keys = jnp.concatenate([keys, ka_ref[...]], axis=1)
    values = jnp.concatenate([own_v[...], other_v[...]], axis=0)
    lane = lax.broadcasted_iota(jnp.int32, (row_tile, LANES), 1)
    for start in range(0, rows, row_tile):
        here = pl.ds(start, row_tile)
        scaled = q_ref[here, :] * jnp.asarray(HEAD_WIDTH**-0.5, BF16)
        marks = qa_ref[here, :]
        halves, lses = [], []
        for which in range(2):
            own = jnp.where(half_lanes(scaled.shape, which), scaled, jnp.zeros_like(scaled))
            scores = cols_of(jnp.concatenate([own, marks], axis=1), keys)
            peak = jnp.max(scores, axis=1, keepdims=True)
            weights = jnp.exp(scores - peak)
            total = jnp.sum(weights, axis=1, keepdims=True)
            halves.append(dot(weights.astype(BF16), values) / total)
            lses.append(peak + jnp.log(total))
        mixed = jnp.where(lane < HEAD_WIDTH, halves[0], halves[1])
        o_ref[here, :] = (mixed * live_ref[here, :]).astype(BF16)
        kept = jnp.where(pair == 0, jnp.zeros((row_tile, LANES), F32), lse_ref[here, :])
        kept = jnp.where(lane == 2 * pair, lses[0], kept)
        lse_ref[here, :] = jnp.where(lane == 2 * pair + 1, lses[1], kept)


def attention_specs(rows, first):
    per_pair = pl.BlockSpec((rows, LANES), lambda i: (0, i + first))
    two = pl.BlockSpec((2, rows, LANES), lambda i: (0, 0, i + first))
    whole = lambda n: pl.BlockSpec((n, LANES), lambda i: (0, 0))
    return per_pair, two, whole(rows), whole(2 * rows)


def ignoring(kernel, start, count):
    return lambda *refs: kernel(*refs[:start], *refs[start + count :])


def attend_forward(first, pairs_here, q, own_k, own_v, other_k, other_v, q_marks, k_marks, live, after=()):
    rows = q.shape[0]
    per_pair, _, marks, all_marks = attention_specs(rows, first)
    out_pair = attention_specs(rows, 0)[0]
    return pl.pallas_call(
        ignoring(partial(attend_forward_kernel, 4), 8, len(after)),
        grid=(pairs_here,),
        in_specs=[per_pair] * 5 + [marks, all_marks, marks] + [ANY] * len(after),
        out_specs=[out_pair, marks],
        out_shape=[shape((rows, pairs_here * LANES)), shape((rows, LANES), F32)],
        compiler_params=pltpu.CompilerParams(vmem_limit_bytes=16 * MIB),
    )(q, own_k, own_v, other_k, other_v, q_marks, k_marks, live, *after)


def widen_kernel(count, tile, *refs):
    attended_parts, refs = refs[:count], refs[count:]
    x_rows, vec, up_shift, own_out, own_up = refs[:5]
    pieces = refs[5:9]
    attended, branch, middle, normed, active, slope, out_weight, up_weight, out_sems, up_sems = refs[9:]
    out_cols = own_out.shape[1]
    out_copies = stage(out_weight, own_out, pieces, 0, 0, out_sems)
    up_copies = stage(up_weight, own_up, pieces, out_cols, 0, up_sems)
    at = 0
    for part in attended_parts:
        attended[:, at : at + part.shape[1]] = part[...]
        at += part.shape[1]
    wait_all(out_copies)
    rows, width = attended.shape
    for start in range(0, rows, tile):
        here = slice(start, start + tile)
        found = dot(attended[here, :], out_weight[...]) + vector(vec, OUT_BIAS)
        branch[here, :] = found
        mid = x_rows[here, :].astype(F32) + vector(vec, SCALE_ATTN) * found
        middle[here, :] = mid
        xhat, _ = norm_parts(mid)
        normed[here, :] = (xhat * vector(vec, LN2_GAIN) + vector(vec, LN2_BIAS)).astype(BF16)
    wait_all(up_copies)

    def widen(block, _):
        cols = pl.ds(pl.multiple_of(block * width, width), width)
        for start in range(0, rows, tile):
            here = slice(start, start + tile)
            hidden = dot(normed[here, :], up_weight[:, cols]) + up_shift[:, cols]
            bell = jnp.exp(-0.5 * hidden * hidden) * (1 / sqrt(2 * pi))
            below = 0.5 + 0.5 * lax.erf(hidden * sqrt(0.5))
            active[here, cols] = (hidden * below).astype(BF16)
            slope[here, cols] = (below + hidden * bell).astype(BF16)
        return 0

    lax.fori_loop(0, up_weight.shape[1] // width, widen, 0)


def down_terms_kernel(chips, *refs):
    active, vec, cots = refs[0], refs[1], refs[2 : 2 + chips]
    cot_rows, down_in, sums = refs[2 + chips : 5 + chips]
    terms = refs[5 + chips :]
    capacity = cots[0].shape[0]
    bias_sum = None
    for i, part in enumerate(cots):
        here = slice(i * capacity, (i + 1) * capacity)
        cot_rows[here, :] = part[...]
        scaled = (part[...].astype(F32) * vector(vec, SCALE_MLP)).astype(BF16)
        down_in[here, :] = scaled
        term = jnp.sum(scaled.astype(F32), axis=0, keepdims=True)
        bias_sum = term if i == 0 else bias_sum + term
    sums[...] = bias_sum
    emit_terms(active, down_in, None, terms, 0)


def down_kernel(chips, tile, *refs):
    active, slope, middle, cot_rows, down_in, vec, own = refs[:7]
    pieces, refs = refs[7:11], refs[11:]
    outs, refs = refs[:chips], refs[chips:]
    hidden_grad, sums, up_shift_grad, weight, sems = refs
    copies = stage(weight, own, pieces, 0, 0, sems)
    rows, width = middle.shape
    capacity = outs[0].shape[0]
    wait_all(copies)
    scale_sum = None
    for i in range(chips):
        here = slice(i * capacity, (i + 1) * capacity)
        found = dot(active[here, :], weight[...]) + vector(vec, DOWN_BIAS)
        outs[i][...] = (middle[here, :] + vector(vec, SCALE_MLP) * found).astype(BF16)
        term = jnp.sum(cot_rows[here, :].astype(F32) * found, axis=0, keepdims=True)
        scale_sum = term if i == 0 else scale_sum + term
    sums[...] = scale_sum

    def back(block, _):
        cols = pl.ds(pl.multiple_of(block * width, width), width)
        total = None
        for start in range(0, rows, tile):
            here = slice(start, start + tile)
            grad = cols_of(down_in[here, :], weight[cols, :])
            grad = (grad * slope[here, cols].astype(F32)).astype(BF16)
            hidden_grad[here, cols] = grad
            term = jnp.sum(grad.astype(F32), axis=0, keepdims=True)
            total = term if start == 0 else total + term
        up_shift_grad[:, cols] = total
        return 0

    lax.fori_loop(0, hidden_grad.shape[1] // width, back, 0)


def narrow_kernel(tile, *refs):
    hidden_grad, middle, branch, vec, own_out, own_up = refs[:6]
    pieces, cot_rows, refs = refs[6:10], refs[10], refs[11:]
    middle_grad, branch_grad, attended_grad, sums = refs[:4]
    out_weight, up_weight, out_sems, up_sems = refs[4:]
    out_cols = own_out.shape[1]
    up_copies = stage(up_weight, own_up, pieces, out_cols, 0, up_sems)
    out_copies = stage(out_weight, own_out, pieces, 0, 0, out_sems)
    wait_all(up_copies)
    rows = middle.shape[0]
    totals = [None] * 4
    for start in range(0, rows, tile):
        here = slice(start, start + tile)
        grad = cols_of(hidden_grad[here, :], up_weight[...])
        xhat, rstd = norm_parts(middle[here, :])
        mid = cot_rows[here, :].astype(F32) + norm_back(grad * vector(vec, LN2_GAIN), xhat, rstd)
        middle_grad[here, :] = mid
        back = (mid * vector(vec, SCALE_ATTN)).astype(BF16)
        branch_grad[here, :] = back
        for i, term in enumerate((grad * xhat, grad, mid * branch[here, :], back.astype(F32))):
            term = jnp.sum(term, axis=0, keepdims=True)
            totals[i] = term if start == 0 else totals[i] + term
    for i, total in enumerate(totals):
        sums[i : i + 1, :] = total
    wait_all(out_copies)
    for start in range(0, rows, tile):
        here = slice(start, start + tile)
        attended_grad[here, :] = cols_of(branch_grad[here, :], out_weight[...]).astype(BF16)


def up_terms_kernel(hidden_grad, normed, branch_grad, attended, *refs):
    terms, (up_scratch, out_scratch) = refs[:4], refs[4:]
    emit_terms(normed, hidden_grad, up_scratch, terms, 0)
    emit_terms(attended, branch_grad, out_scratch, terms, hidden_grad.shape[1])


def attend_backward_kernel(
    tiles,
    skipped,
    q_ref,
    own_k,
    own_v,
    other_k,
    other_v,
    qa_ref,
    ka_ref,
    live_ref,
    o_ref,
    lse_ref,
    g_ref,
    dq_ref,
    own_grad_ref,
    other_grad_ref,
    dk_sum,
    dv_sum,
):
    pair = pl.program_id(0) + skipped
    rows = q_ref.shape[0]
    row_tile = rows // tiles
    key_rows = jnp.concatenate([own_k[...], other_k[...]], axis=0)
    keys = jnp.concatenate([key_rows, ka_ref[...]], axis=1)
    values = jnp.concatenate([own_v[...], other_v[...]], axis=0)
    lane = lax.broadcasted_iota(jnp.int32, (row_tile, LANES), 1)
    scale = HEAD_WIDTH**-0.5
    for start in range(0, rows, row_tile):
        here = pl.ds(start, row_tile)
        scaled = q_ref[here, :] * jnp.asarray(scale, BF16)
        marks = qa_ref[here, :]
        grads = (g_ref[here, :] * live_ref[here, :]).astype(BF16)
        both = grads.astype(F32) * o_ref[here, :].astype(F32)
        halves = []
        key_part = value_part = None
        for which in range(2):
            mine = half_lanes(scaled.shape, which)
            own = jnp.where(mine, scaled, jnp.zeros_like(scaled))
            own_grads = jnp.where(mine, grads, jnp.zeros_like(grads))
            row_dot = jnp.sum(jnp.where(mine, both, 0.0), axis=1, keepdims=True)
            lse = jnp.sum(
                jnp.where(lane == 2 * pair + which, lse_ref[here, :], 0.0), axis=1, keepdims=True
            )
            scores = cols_of(jnp.concatenate([own, marks], axis=1), keys)
            probs = jnp.exp(scores - lse)
            prob_grads = cols_of(own_grads, values)
            score_grads = (probs * (prob_grads - row_dot)).astype(BF16)
            halves.append(dot(score_grads, key_rows))
            value_term = rows_of(probs.astype(BF16), own_grads)
            key_term = rows_of(score_grads, own)
            value_part = value_term if which == 0 else value_part + value_term
            key_part = key_term if which == 0 else key_part + key_term
        mixed = jnp.where(lane < HEAD_WIDTH, halves[0], halves[1])
        dq_ref[here, :] = (mixed * scale).astype(BF16)
        if start == 0:
            dk_sum[...] = key_part
            dv_sum[...] = value_part
        else:
            dk_sum[...] += key_part
            dv_sum[...] += value_part
    own_grad_ref[0] = dk_sum[:rows, :].astype(BF16)
    own_grad_ref[1] = dv_sum[:rows, :].astype(BF16)
    other_grad_ref[0] = dk_sum[rows:, :].astype(BF16)
    other_grad_ref[1] = dv_sum[rows:, :].astype(BF16)


def attend_backward(
    first, pairs_here, skipped, q, own_k, own_v, other_k, other_v, q_marks, k_marks, live, attended, lse, grads, after=()
):
    rows = q.shape[0]
    per_pair, _, marks, all_marks = attention_specs(rows, first)
    out_pair, out_two = attention_specs(rows, 0)[:2]
    there = attention_specs(rows, skipped)[0]
    return pl.pallas_call(
        ignoring(partial(attend_backward_kernel, 4, skipped), 11, len(after)),
        grid=(pairs_here,),
        in_specs=[per_pair] * 5 + [marks, all_marks, marks, there, marks, per_pair]
        + [ANY] * len(after),
        out_specs=[out_pair, out_two, out_two],
        out_shape=[shape((rows, pairs_here * LANES))]
        + [shape((2, rows, pairs_here * LANES))] * 2,
        scratch_shapes=[pltpu.VMEM((2 * rows, LANES), F32)] * 2,
        compiler_params=pltpu.CompilerParams(vmem_limit_bytes=16 * MIB),
    )(q, own_k, own_v, other_k, other_v, q_marks, k_marks, live, attended, lse, grads, *after)


def emit_terms(left, right, scratch, terms, at):
    away, keep, keep_far, keep_own = terms
    mine, core = lax.axis_index("fsdp"), lax.axis_index("seq") % 2
    count, cols = left.shape[1] // 4, right.shape[1]
    half = count // 2
    here = slice(at, at + cols)
    if scratch is not None:
        scratch[...] = rows_of(left[...], right[...])

    def rows_at(flip, which):
        start = (mine ^ flip) * count + which * half
        if scratch is not None:
            value = scratch[pl.ds(pl.multiple_of(start, 16), half), :]
        else:
            value = rows_of(left[:, pl.ds(pl.multiple_of(start, LANES), half)], right[...])
        return value.astype(BF16)

    for i in range(2):
        home = core ^ i
        rows = [rows_at(1 + home, home), rows_at(1 + home, 1 - home), rows_at(3, home), rows_at(0, home)]
        if i == 0:
            keep[:half, here] = rows[0]
            keep[half:, here] = rows[1]
            keep_far[:, here] = rows[2]
            keep_own[:, here] = rows[3]
        else:
            for j, value in enumerate(rows):
                away[j * half : (j + 1) * half, here] = value


def term_shapes(rows, cols):
    return [shape((count, cols)) for count in (2 * rows, rows, rows // 2, rows // 2)]


class Reduction:
    def __init__(self, terms):
        self.away, self.keep, self.keep_far, self.keep_own = terms
        self.count = self.keep_far.shape[0]

    def send_other(self):
        self.other = to_core(self.away)
        return [self.other]

    def send_far(self):
        part = self.other[2 * self.count : 3 * self.count]
        self.far = to_fsdp((wide(self.keep_far) + wide(part)).astype(BF16), (2, 1))
        return [self.far]

    def send_near(self):
        first = wide(self.keep[: self.count]) + wide(self.other[: self.count]) + wide(self.far)
        second = wide(self.keep[self.count :]) + wide(self.other[self.count : 2 * self.count])
        self.near = to_fsdp(jnp.concatenate([first, second], 0).astype(BF16), (1, 2))
        return [self.near]

    def send_both(self):
        self.both = to_core(self.near[self.count :])
        return [self.both]

    def send_chips(self):
        flips = [1 << i for i in range((lax.axis_size("seq") // 2).bit_length() - 1)]
        self.orders = list(zip(flips, flips[::-1]))
        total = wide(self.keep_own) + wide(self.other[3 * self.count :])
        self.sent = (total + wide(self.near[: self.count]) + wide(self.both)).astype(BF16)
        self.got = to_chip(self.sent, *self.orders[0])
        return [self.got]

    def send_chips_again(self):
        for order in self.orders[1:]:
            self.sent = (wide(self.sent) + wide(self.got)).astype(BF16)
            self.got = to_chip(self.sent, *order)
        return [self.got]

    def send_total(self):
        self.total = (wide(self.sent) + wide(self.got)).astype(BF16)
        self.other_total = to_core(self.total)
        return [self.other_total]

    def shards(self, widths, after=()):
        outs = [shape((2 * self.count, cols), F32) for cols in widths]
        operands = [(self.total, VMEM), (self.other_total, VMEM)]
        return call(spread_kernel, operands, outs, after=after)


def spread_kernel(own_ref, other_ref, *outs):
    core = lax.axis_index("seq") % 2
    half = own_ref.shape[0]
    at = 0
    for out in outs:
        cols = out.shape[1]
        for i, source in enumerate((own_ref, other_ref)):
            start = pl.multiple_of((core ^ i) * half, 16)
            out[pl.ds(start, half), :] = source[:, at : at + cols].astype(F32)
        at += cols


def project_grad_kernel(count, *refs):
    q_grads, own_grads, other_grads = refs[:count], refs[count : 2 * count], refs[2 * count : 3 * count]
    normed, projected_grad, sums = refs[3 * count : 3 * count + 3]
    terms, scratch = refs[3 * count + 3 : 3 * count + 7], refs[3 * count + 7]
    width = normed.shape[1]
    at = 0
    for q_grad, own_grad, other_grad in zip(q_grads, own_grads, other_grads):
        here = slice(at, at + q_grad.shape[1])
        projected_grad[:, here] = q_grad[...]
        sums[0:1, here] = jnp.sum(q_grad[...].astype(F32), axis=0, keepdims=True)
        for i in range(2):
            both = (own_grad[i].astype(F32) + other_grad[i].astype(F32)).astype(BF16)
            first = (i + 1) * width + at
            projected_grad[:, first : first + q_grad.shape[1]] = both
        sums[1:2, here] = jnp.sum(both.astype(F32), axis=0, keepdims=True)
        at += q_grad.shape[1]
    emit_terms(normed, projected_grad, scratch, terms, 0)


def input_kernel(chips, *refs):
    projected_grad, x_rows, middle_grad, vec = refs[:4]
    qkv_sums, narrow_sums, down_shift_grad, scale_grad, up_shift_grad, own = refs[4:10]
    pieces, rest = refs[10:14], refs[14:]
    outs, sums, weight, sems = rest[:chips], rest[chips], rest[chips + 1], rest[chips + 2]
    copies = stage(weight, own, pieces, 0, EXTRA_ROWS, sems)
    capacity, width = outs[0].shape
    wait_all(copies)
    totals = [None] * 2
    for i in range(chips):
        here = slice(i * capacity, (i + 1) * capacity)
        grad = cols_of(projected_grad[here, :], weight[...])
        xhat, rstd = norm_parts(x_rows[here, :].astype(F32))
        back = norm_back(grad * vector(vec, LN1_GAIN), xhat, rstd)
        outs[i][...] = (middle_grad[here, :] + back).astype(BF16)
        for j, term in enumerate((grad * xhat, grad)):
            term = jnp.sum(term, axis=0, keepdims=True)
            totals[j] = term if i == 0 else totals[j] + term
    sums[...] = jnp.zeros_like(sums)
    for row, value in (
        (LN1_GAIN, totals[0]),
        (LN1_BIAS, totals[1]),
        (QUERY_BIAS, qkv_sums[0:1, :]),
        (VALUE_BIAS, qkv_sums[1:2, :]),
        (OUT_BIAS, narrow_sums[3:4, :]),
        (SCALE_ATTN, narrow_sums[2:3, :]),
        (LN2_GAIN, narrow_sums[0:1, :]),
        (LN2_BIAS, narrow_sums[1:2, :]),
        (DOWN_BIAS, down_shift_grad[...]),
        (SCALE_MLP, scale_grad[...]),
    ):
        sums[row : row + 1, :] = value
    for f in range(4):
        sums[UP_ROW + f : UP_ROW + f + 1, :] = up_shift_grad[:, f * width : (f + 1) * width]


def body(
    tokens,
    image_tokens,
    ln1_gain,
    ln1_bias,
    qkv_weight,
    query_bias,
    value_bias,
    out_weight,
    out_bias,
    scale_attn,
    ln2_gain,
    ln2_bias,
    up_weight,
    up_bias,
    down_weight,
    down_bias,
    scale_mlp,
    cotangent,
):
    seq_count = lax.axis_size("seq")
    fsdp_index = lax.axis_index("fsdp")
    chips = seq_count // 2
    micro_count, tok_count, width = tokens.shape[0], tokens.shape[2], tokens.shape[4]
    slots, images = image_tokens.shape[2:]
    assert chips == micro_count * slots and lax.axis_size("fsdp") == 4
    assert slots * images < PAD_SEGMENT
    capacity = ceil_to((LONG - 2) // seq_count + 2, 16)
    rows = chips * capacity
    tile = rows // 2
    hidden_width = up_weight.shape[1]
    sizes = (slots, images, chips, capacity, tok_count, seq_count)
    counts = image_tokens

    def prepare(values, groups, small=(), after=(), send=True):
        flat = values.reshape(micro_count * tok_count, width)
        shards = [shard for group in groups for shard in group]
        more = EXTRA_ROWS if small else 0
        outs = [
            shape((group[0].shape[0] + more, sum(shard.shape[1] for shard in group)))
            for group in groups
        ]
        if small:
            outs += [shape((outs[0].shape[0] // 2 + more // 2, outs[0].shape[1]))]
        else:
            outs += [shape((rows, LANES)), shape((2 * rows, LANES)), shape((rows, LANES), F32)]
        results = call(
            partial(prepare_kernel, sizes, [len(group) for group in groups], len(small)),
            [(counts, SMEM)] + [(item, VMEM) for item in [flat] + shards + list(small)],
            [shape((capacity, width))] * chips + outs,
            [pltpu.VMEM((EXTRA_ROWS, width), F32)] if small else [],
            after=after,
            limit=60 if small else 16,
        )
        parts = list(results[:chips])
        if send:
            for label in range(chips - 1, 0, -1):
                parts[label] = to_chip(parts[label], *flips_of(label, chips))
        return parts, *results[chips:]

    def cross(parts, bit):
        labels = [label for label in range(chips) if label & bit]
        return to_chip(jnp.concatenate([parts[label] for label in labels]), *flips_of(bit, chips))

    def crossed(parts, moved, bit):
        parts = list(parts)
        for i, label in enumerate(label for label in range(chips) if label & bit):
            parts[label] = moved[i * capacity : (i + 1) * capacity]
        return parts

    def cross_rest(parts):
        bit = 2
        while 2 * bit < chips:
            parts = crossed(parts, cross(parts, bit), bit)
            bit *= 2
        return parts, cross(parts, bit), bit

    def collect(parts, after=()):
        return call(
            partial(collect_kernel, sizes),
            [(counts, SMEM)] + [(part, VMEM) for part in parts],
            [shape((micro_count * tok_count, width))],
            after=after,
        )[0]

    small = [
        ln1_gain,
        ln1_bias,
        query_bias,
        value_bias,
        out_bias,
        scale_attn,
        ln2_gain,
        ln2_bias,
        down_bias,
        scale_mlp,
    ]
    own_rows = ln1_gain.shape[0]
    x_parts, qkv_sent, qkv_first = prepare(tokens, [[qkv_weight]], small + [up_bias])
    near, far = to_fsdp(qkv_sent, (1, 2)), to_fsdp(qkv_first, (3, 3))
    cot_sent, up_sent, down_sent, q_marks, k_marks, live = prepare(
        cotangent, [[out_weight, up_weight], [down_weight]], after=[qkv_sent], send=False
    )
    near, far, up_sent = hold([near, far, up_sent], x_parts + [q_marks])
    qkv_pieces = [near, to_core(near), far, to_core(far)]
    up_near = to_fsdp(up_sent, (1, 2))

    x_rows, normed_first, q, own_k, own_v, vec, up_shift = call(
        partial(project_kernel, chips),
        [(part, VMEM) for part in x_parts]
        + [(item, ANY) for item in [qkv_sent, qkv_weight] + qkv_pieces],
        [shape((rows, width))] * 5
        + [shape((EXTRA_ROWS, width), F32), shape((1, hidden_width), F32)],
        [
            pltpu.VMEM((width, 3 * width), BF16),
            pltpu.VMEM((4, EXTRA_ROWS, width), BF16),
            STAGE_SEMS,
            pltpu.SemaphoreType.DMA((4,)),
        ],
    )
    down_sent, *cot_sent = hold([down_sent] + cot_sent, [q])
    down_near = to_fsdp(down_sent, (1, 2))
    cot_moved = cross(cot_sent, 1)
    attention = (q, own_k, own_v, to_core(own_k), to_core(own_v), q_marks, k_marks, live)
    step = width // LANES // 3
    attended_parts, lses = [], []

    def forward(i):
        part, lse = attend_forward(i * step, step, *attention, after=attended_parts[-1:])
        attended_parts.append(part)
        lses.append(lse)
        return part

    up_near, cot_moved = hold([up_near, cot_moved], [forward(0)])
    cot_parts = crossed(cot_sent, cot_moved, 1)
    up_far = to_fsdp(up_near[: own_rows // 2], (2, 1))
    cot_parts, cot_moved, last_bit = cross_rest(cot_parts)
    up_far, down_near, cot_moved = hold([up_far, down_near, cot_moved], [forward(1)])
    cot_parts = crossed(cot_parts, cot_moved, last_bit)
    up_pieces = [up_near, to_core(up_near), up_far, to_core(up_far)]
    down_far = to_fsdp(down_near[: down_weight.shape[0] // 2], (2, 1))
    up_pieces = hold(up_pieces, [forward(2)])
    (down_near,) = hold([down_near], up_pieces)
    down_other = to_core(down_near)

    up_scratch = [
        pltpu.VMEM((width, width), BF16),
        pltpu.VMEM((width, hidden_width), BF16),
        STAGE_SEMS,
        STAGE_SEMS,
    ]
    attended, branch, middle, normed_second, active, slope = call(
        partial(widen_kernel, len(attended_parts), tile),
        [(item, VMEM) for item in attended_parts + [x_rows, vec, up_shift]]
        + [(item, ANY) for item in [out_weight, up_weight] + up_pieces],
        [
            shape((rows, width)),
            shape((rows, width), F32),
            shape((rows, width), F32),
            shape((rows, width)),
            shape((rows, hidden_width)),
            shape((rows, hidden_width)),
        ],
        up_scratch,
    )
    down_far, down_other = hold([down_far, down_other], [attended])
    far_other = to_core(down_far)
    cot_rows, down_in, down_shift_grad, *down_terms = call(
        partial(down_terms_kernel, chips),
        [(item, VMEM) for item in [active, vec] + cot_parts],
        [shape((rows, width)), shape((rows, width)), shape((1, width), F32)]
        + term_shapes(down_weight.shape[0], width),
        after=[down_far],
    )
    down = Reduction(down_terms)
    down_pieces = [down_near, down_other, down_far, far_other]
    down.away, *down_pieces = hold([down.away] + down_pieces, [down_in])
    waits = down.send_other()
    results = call(
        partial(down_kernel, chips, tile),
        [(item, VMEM) for item in (active, slope, middle, cot_rows, down_in, vec)]
        + [(item, ANY) for item in [down_weight] + down_pieces],
        [shape((capacity, width))] * chips
        + [
            shape((rows, hidden_width)),
            shape((1, width), F32),
            shape((1, hidden_width), F32),
        ],
        [pltpu.VMEM((hidden_width, width), BF16), STAGE_SEMS],
    )
    out_sent, (hidden_grad, scale_grad, up_shift_grad) = list(results[:chips]), results[chips:]
    (down.other,) = hold(waits, [hidden_grad])
    waits = down.send_far()

    middle_grad, branch_grad, attended_grad, narrow_sums = call(
        partial(narrow_kernel, tile),
        [(item, VMEM) for item in (hidden_grad, middle, branch, vec)]
        + [(item, ANY) for item in [out_weight, up_weight] + up_pieces]
        + [(cot_rows, VMEM)],
        [
            shape((rows, width), F32),
            shape((rows, width)),
            shape((rows, width)),
            shape((4, width), F32),
        ],
        up_scratch,
    )
    down.far, *out_sent = hold(waits + out_sent, [middle_grad])
    waits = down.send_near()
    out_moved = cross(out_sent, 1)
    up_terms = call(
        up_terms_kernel,
        [(item, VMEM) for item in (hidden_grad, normed_second, branch_grad, attended)],
        term_shapes(own_rows, hidden_width + width),
        [pltpu.VMEM((width, hidden_width), F32), pltpu.VMEM((width, width), F32)],
    )
    up = Reduction(up_terms)

    query_grads, own_grads, other_grads = [], [], []

    def backward(first, after=()):
        query_grad, own_grad, other_grad = attend_backward(
            first,
            1,
            first % step,
            *attention,
            attended_parts[first // step],
            lses[first // step],
            attended_grad,
            after=query_grads[-1:] + list(after),
        )
        query_grads.append(query_grad)
        own_grads.append(own_grad)
        other_grads.append(other_grad)
        return query_grad

    def hold_grads(arrays):
        first, count = sent_grads[0], len(arrays)
        items = hold(list(arrays) + other_grads[first:], query_grads[-1:])
        other_grads[first:] = items[count:]
        sent_grads[0] = len(other_grads)
        return items[:count], [to_core(item) for item in other_grads[first:]]

    sent_grads = [0]
    core_grads = []

    backward(0, up_terms[:1])
    (down.near, up.away, out_moved), moved = hold_grads(waits + [up.away, out_moved])
    out_parts = crossed(out_sent, out_moved, 1)
    waits = down.send_both() + up.send_other() + moved
    out_parts, out_moved, _ = cross_rest(out_parts)
    backward(1)
    (down.both, up.other, *core_grads), fresh = hold_grads(waits)
    waits = down.send_chips() + up.send_far() + [out_moved] + fresh
    backward(2)
    backward(3)
    (down.got, up.far, out_moved, *more), fresh = hold_grads(waits)
    out_parts = crossed(out_parts, out_moved, last_bit)
    core_grads += more
    waits = up.send_near() + down.send_chips_again() + fresh
    backward(4)
    backward(5)
    (up.near, down.got, *more), fresh = hold_grads(waits)
    core_grads += more
    (up.both, *more) = hold(up.send_both() + fresh, [])
    core_grads += more
    got = up.send_chips()
    waits = down.send_total()

    projected_grad, qkv_sums, *qkv_terms = call(
        partial(project_grad_kernel, len(query_grads)),
        [(item, VMEM) for item in query_grads + own_grads + core_grads + [normed_first]],
        [shape((rows, 3 * width)), shape((2, width), F32)] + term_shapes(own_rows, 3 * width),
        [pltpu.VMEM((width, 3 * width), F32)],
    )
    output = collect(out_parts, [projected_grad])
    (down.other_total,) = hold(waits, [output])
    (down_grad,) = down.shards([width])
    qkv = Reduction(qkv_terms)
    (qkv.away,) = hold([qkv.away], [projected_grad])
    (qkv.other,) = hold(qkv.send_other(), [])
    waits = qkv.send_far()
    *in_sent, sums = call(
        partial(input_kernel, chips),
        [(item, VMEM) for item in (projected_grad, x_rows, middle_grad, vec)]
        + [(item, VMEM) for item in (qkv_sums, narrow_sums, down_shift_grad, scale_grad, up_shift_grad)]
        + [(item, ANY) for item in [qkv_weight] + qkv_pieces],
        [shape((capacity, width))] * chips + [shape((EXTRA_ROWS, width), F32)],
        [pltpu.VMEM((width, 3 * width), BF16), STAGE_SEMS],
    )
    qkv.far, up.got, sums, *in_sent = hold(waits + got + [sums] + in_sent, [down_grad])
    waits = qkv.send_near()
    got = up.send_chips_again()
    in_moved = cross(in_sent, 1)
    other_sums = to_core(sums)
    qkv.near, sums, other_sums, in_moved = hold(waits + [sums, other_sums, in_moved], [])
    sums = sums + other_sums
    other_sums = to_fsdp(sums, (1, 1))
    in_parts, in_moved, _ = cross_rest(crossed(in_sent, in_moved, 1))
    (qkv.both,) = hold(qkv.send_both(), [])
    waits = qkv.send_chips()
    qkv.got, up.got, sums, other_sums = hold(waits + got + [sums, other_sums], [])
    sums = sums + other_sums
    other_sums = to_fsdp(sums, (2, 2))
    waits = qkv.send_chips_again()
    (in_moved,) = hold([in_moved], [])
    input_grad = collect(crossed(in_parts, in_moved, last_bit))
    up.send_total()
    up_grad, out_grad = up.shards([hidden_width, width])
    qkv.got, sums, other_sums = hold(waits + [sums, other_sums], [input_grad, up_grad])
    sums = sums + other_sums
    flip = 1
    while flip < chips:
        sums = sums + to_chip(sums, flip)
        flip *= 2
    qkv.send_total()
    (qkv_grad,) = qkv.shards([3 * width])
    output, input_grad = output.reshape(tokens.shape), input_grad.reshape(tokens.shape)

    small_grads = lax.dynamic_slice_in_dim(sums[:UP_ROW], fsdp_index * own_rows, own_rows, 1)
    up_shift_total = lax.dynamic_index_in_dim(sums, UP_ROW + fsdp_index, 0, keepdims=False)
    return (
        output,
        input_grad,
        small_grads[LN1_GAIN],
        small_grads[LN1_BIAS],
        qkv_grad,
        small_grads[QUERY_BIAS],
        small_grads[VALUE_BIAS],
        out_grad,
        small_grads[OUT_BIAS],
        small_grads[SCALE_ATTN],
        small_grads[LN2_GAIN],
        small_grads[LN2_BIAS],
        up_grad,
        up_shift_total,
        down_grad,
        small_grads[DOWN_BIAS],
        small_grads[SCALE_MLP],
    )


def solution(mesh):
    vector, matrix = P("fsdp"), P("fsdp", None)
    places = P(None, "fsdp", None, "seq", None)
    return jax.shard_map(
        body,
        mesh=mesh,
        in_specs=(
            places,
            P(None, "fsdp", None, None),
            vector,
            vector,
            matrix,
            vector,
            vector,
            matrix,
            vector,
            vector,
            vector,
            vector,
            matrix,
            vector,
            matrix,
            vector,
            vector,
            places,
        ),
        out_specs=(
            places,
            places,
            vector,
            vector,
            matrix,
            vector,
            vector,
            matrix,
            vector,
            vector,
            vector,
            vector,
            matrix,
            vector,
            matrix,
            vector,
            vector,
        ),
        check_vma=False,
    )
```

```python
from functools import partial
from math import pi, sqrt

import jax
import jax.numpy as jnp
from jax import lax
from jax.experimental import pallas as pl
from jax.experimental.pallas import tpu as pltpu
from jax.sharding import PartitionSpec as P

LONG = 1029
EPSILON = 1e-06
MASK_VALUE = -1e30
PAD_SEGMENT = 127
LANES = 128
HEAD_WIDTH = 64
MIB = 2**20
BOTH = ("fsdp", "seq")
F32 = jnp.float32
BF16 = jnp.bfloat16
VMEM = pl.BlockSpec()
SMEM = pl.BlockSpec(memory_space=pltpu.SMEM)
ANY = pl.BlockSpec(memory_space=pl.ANY)

LN1_GAIN, LN1_BIAS, QUERY_BIAS, VALUE_BIAS, OUT_BIAS = 0, 1, 2, 3, 4
SCALE_ATTN, LN2_GAIN, LN2_BIAS, DOWN_BIAS, SCALE_MLP, UP_ROW = 5, 6, 7, 8, 9, 10


def ceil_to(value, step):
    return (value + step - 1) // step * step


def move(value, flips):
    fsdp_count, seq_count = lax.axis_size("fsdp"), lax.axis_size("seq")
    pairs = []
    for f in range(fsdp_count):
        for s in range(seq_count):
            fsdp_flip, chip_flip, core_flip = flips[s % 2]
            there = (f ^ fsdp_flip) * seq_count + (s ^ (2 * chip_flip + core_flip))
            pairs.append((f * seq_count + s, there))
    return lax.ppermute(value, BOTH, pairs)


def to_core(value):
    return move(value, [(0, 0, 1)] * 2)


def to_chip(value, flip, other_flip=None):
    return move(value, [(0, flip, 0), (0, flip if other_flip is None else other_flip, 0)])


def to_fsdp(value, flips):
    return move(value, [(flip, 0, 0) for flip in flips])


def wide(value):
    return value.astype(F32)


def dot(left, right):
    return jnp.dot(left, right, preferred_element_type=F32)


def rows_of(left, right):
    return lax.dot_general(left, right, (((0,), (0,)), ((), ())), preferred_element_type=F32)


def cols_of(left, right):
    return lax.dot_general(left, right, (((1,), (1,)), ((), ())), preferred_element_type=F32)


def shape(dims, dtype=BF16):
    return jax.ShapeDtypeStruct(dims, dtype)


def call(kernel, operands, outs, scratch=(), after=(), limit=16, aliases=None):
    count = len(operands)

    def run(*refs):
        kernel(*refs[:count], *refs[count + len(after) :])

    return pl.pallas_call(
        run,
        in_specs=[spec for _, spec in operands] + [ANY] * len(after),
        out_specs=[ANY if aliases else VMEM] * len(outs),
        out_shape=list(outs),
        scratch_shapes=list(scratch),
        input_output_aliases=aliases or {},
        compiler_params=pltpu.CompilerParams(vmem_limit_bytes=limit * MIB),
    )(*[array for array, _ in operands], *after)


def hold(arrays, after):
    results = call(
        lambda *refs: None,
        [(item, ANY) for item in arrays],
        [shape(item.shape, item.dtype) for item in arrays],
        after=after,
        aliases={i: i for i in range(len(arrays))},
    )
    return list(results)


def flips_of(label, chips):
    bits = chips.bit_length() - 1
    return sum(((label >> i) & 1) << (bits - 1 - i) for i in range(bits)), label


def flip_of(label, core, chips):
    first, second = flips_of(label, chips)
    return label if first == second else jnp.where(core == 0, first, second)


def places_of(counts_ref, slots, images, chip, source, tok_count, seq_count):
    micro, slot = chip // slots, chip % slots
    total = jnp.int32(0)
    ends, sizes = [], []
    for j in range(slots):
        size = jnp.int32(0)
        for i in range(images):
            size = size + counts_ref[micro, 0, j, i]
            ends.append(total + size)
        sizes.append(size)
        total = total + size
    free = seq_count * tok_count - total
    start, room_end = jnp.int32(0), jnp.int32(0)
    picked = [jnp.int32(0)] * 4
    for j in range(slots):
        room = LONG - sizes[j]
        span = (
            start,
            start + sizes[j],
            total + jnp.minimum(room_end, free),
            total + jnp.minimum(room_end + room, free),
        )
        picked = [jnp.where(slot == j, a, b) for a, b in zip(span, picked)]
        start, room_end = start + sizes[j], room_end + room
    first, last, more, stop = [(a - source + seq_count - 1) // seq_count for a in picked]
    return micro, first, last - first, more, stop - more, total, ends


def local_rows_of(step, first, count, more, extra):
    local = jnp.where(step < count, first + step, more + step - count)
    return local, step < count + extra


def pick_kernel(sizes, counts_ref, values, *parts):
    slots, images, chips, capacity, tok_count, seq_count = sizes
    seq_index = lax.axis_index("seq")
    chip, core = seq_index // 2, seq_index % 2
    for label in range(chips):
        flip = flip_of(label, core, chips)
        micro, first, count, more, extra, _, _ = places_of(
            counts_ref, slots, images, chip ^ flip, seq_index, tok_count, seq_count
        )
        step = lax.broadcasted_iota(jnp.int32, (capacity, tok_count), 0)
        held = lax.broadcasted_iota(jnp.int32, (capacity, tok_count), 1)
        local, valid = local_rows_of(step, first, count, more, extra)
        pick = jnp.where(valid & (local == held), 1.0, 0.0).astype(BF16)
        start = pl.multiple_of(micro * tok_count, tok_count)
        parts[label][...] = dot(pick, values[pl.ds(start, tok_count), :]).astype(BF16)


def line_up_kernel(groups, small_count, *refs):
    shards, refs = refs[: sum(groups)], refs[sum(groups) :]
    smalls, refs = refs[:small_count], refs[small_count:]
    halves, rest = refs[: len(groups)], refs[len(groups) :]
    core = lax.axis_index("seq") % 2
    if smalls:
        first_half, inserted = rest
        half = (halves[0].shape[0] - EXTRA_ROWS) // 2
        inserted[...] = jnp.zeros_like(inserted)
        for i, small in enumerate(smalls):
            length = small.shape[0]
            inserted[i : i + 1, :length] = small[...].astype(F32).reshape(1, length)
        halves[0][half : half + EXTRA_ROWS, : inserted.shape[1]] = inserted[...].astype(BF16)
    at = 0
    for count, out in zip(groups, halves):
        half = shards[at].shape[0] // 2
        for i in range(2):
            start = pl.multiple_of((core ^ i) * half, 16)
            row = i * (out.shape[0] - half)
            col = 0
            for shard in shards[at : at + count]:
                out[row : row + half, col : col + shard.shape[1]] = shard[pl.ds(start, half), :]
                col += shard.shape[1]
        at += count
    if smalls:
        first_half[...] = halves[0][: first_half.shape[0], :]


def collect_kernel(sizes, counts_ref, *refs):
    slots, images, chips, capacity, tok_count, seq_count = sizes
    parts, out = refs[:chips], refs[chips]
    seq_index = lax.axis_index("seq")
    micros = chips // slots
    sums = [None] * micros
    for label in range(chips):
        flip = flip_of(label, seq_index % 2, chips)
        micro, first, count, more, extra, _, _ = places_of(
            counts_ref, slots, images, seq_index // 2 ^ flip, seq_index, tok_count, seq_count
        )
        step = lax.broadcasted_iota(jnp.int32, (tok_count, capacity), 1)
        held = lax.broadcasted_iota(jnp.int32, (tok_count, capacity), 0)
        local, valid = local_rows_of(step, first, count, more, extra)
        pick = jnp.where(valid & (local == held), 1.0, 0.0).astype(BF16)
        found = dot(pick, parts[label][...])
        for m in range(micros):
            term = jnp.where(micro == m, found, 0.0)
            sums[m] = term if sums[m] is None else sums[m] + term
    for m in range(micros):
        out[m * tok_count : (m + 1) * tok_count, :] = sums[m].astype(BF16)


def marks_kernel(sizes, counts_ref, q_marks, k_marks, live_ref):
    slots, images, chips, capacity, tok_count, seq_count = sizes
    rows = chips * capacity
    seq_index = lax.axis_index("seq")
    chip, core = seq_index // 2, seq_index % 2
    row = lax.broadcasted_iota(jnp.int32, (rows, LANES), 0)
    lane = lax.broadcasted_iota(jnp.int32, (rows, LANES), 1)
    for which in range(2):
        segment = jnp.full((rows, LANES), PAD_SEGMENT, jnp.int32)
        live = jnp.zeros((rows, LANES), jnp.int32)
        for label in range(chips):
            flip = flip_of(label, core ^ which, chips)
            source = 2 * (chip ^ flip) + (core ^ which)
            _, first, count, more, extra, total, ends = places_of(
                counts_ref, slots, images, chip, source, tok_count, seq_count
            )
            step = row - label * capacity
            local, valid = local_rows_of(step, first, count, more, extra)
            valid = valid & (step >= 0) & (step < capacity)
            place = local * seq_count + source
            image = jnp.zeros((rows, LANES), jnp.int32)
            for end in ends:
                image = image + (end <= place).astype(jnp.int32)
            segment = jnp.where(valid, image, segment)
            live = jnp.where(valid & (place < total), 1, live)
        same = segment == lane
        k_marks[which * rows : (which + 1) * rows, :] = jnp.where(same, 0.0, MASK_VALUE).astype(
            BF16
        )
        if which == 0:
            q_marks[...] = jnp.where(same, 1.0, 0.0).astype(BF16)
            live_ref[...] = live.astype(F32)


def stage(out, own, pieces, first_col, extra, sems):
    rows, cols = own.shape
    half = rows // 2
    mine, core = lax.axis_index("fsdp"), lax.axis_index("seq") % 2
    copies = []

    def put(source, flip, at):
        start = pl.multiple_of((mine ^ flip) * rows + at, 16)
        copy = pltpu.make_async_copy(
            source, out.at[pl.ds(start, source.shape[0])], sems.at[len(copies)]
        )
        copy.start()
        copies.append(copy)

    here = slice(first_col, first_col + cols)
    put(own, 0, 0)
    for i in range(2):
        home = core ^ i
        near, far = pieces[i], pieces[2 + i]
        put(near.at[:half, here], 1 + home, home * half)
        put(near.at[half + extra :, here], 1 + home, (1 - home) * half)
        put(far.at[:half, here], 3, home * half)
    return copies


def wait_all(copies):
    for copy in copies:
        copy.wait()


STAGE_SEMS = pltpu.SemaphoreType.DMA((7,))
EXTRA_ROWS = 16
ROW_TILE = 640


def norm_parts(values):
    center = values - jnp.mean(values, axis=-1, keepdims=True)
    rstd = lax.rsqrt(jnp.mean(center * center, axis=-1, keepdims=True) + EPSILON)
    return center * rstd, rstd


def norm_back(e, xhat, rstd):
    return rstd * (
        e
        - jnp.mean(e, axis=-1, keepdims=True)
        - xhat * jnp.mean(e * xhat, axis=-1, keepdims=True)
    )


def vector(ref, row):
    return ref[row : row + 1, :]


def project_kernel(chips, *refs):
    x_parts, sent, own, pieces = refs[:chips], refs[chips], refs[chips + 1], refs[chips + 2 : chips + 6]
    x_rows, normed, q, k, v, vec, up_shift, weight, vectors, sems, vector_sems = refs[chips + 6 :]
    copies = stage(weight, own, pieces, 0, EXTRA_ROWS, sems)
    capacity, width = x_parts[0].shape
    half = own.shape[0] // 2
    mine, core = lax.axis_index("fsdp"), lax.axis_index("seq") % 2
    vector_copies = []
    for i, (source, flip) in enumerate(
        ((sent, 0), (pieces[0], 1 + core), (pieces[1], 2 - core), (pieces[2], 3))
    ):
        copy = pltpu.make_async_copy(
            source.at[half : half + EXTRA_ROWS, :width], vectors.at[mine ^ flip], vector_sems.at[i]
        )
        copy.start()
        vector_copies.append(copy)
    wait_all(vector_copies)
    shard = width // 4
    for f in range(4):
        row = lax.broadcasted_iota(jnp.int32, (shard, width), 0)
        col = lax.broadcasted_iota(jnp.int32, (shard, width), 1)
        shift = jnp.where(col == row + f * shard, 1.0, 0.0).astype(BF16)
        placed = dot(vectors[f, :, :shard], shift)
        vec[...] = placed if f == 0 else vec[...] + placed
        up_shift[:, f * width : (f + 1) * width] = vectors[f, UP_ROW : UP_ROW + 1, :].astype(F32)
    for i, part in enumerate(x_parts):
        here = slice(i * capacity, (i + 1) * capacity)
        x_rows[here, :] = part[...]
        xhat, _ = norm_parts(part[...].astype(F32))
        normed[here, :] = (xhat * vector(vec, LN1_GAIN) + vector(vec, LN1_BIAS)).astype(BF16)
    wait_all(copies)
    q[...] = (dot(normed[...], weight[:, :width]) + vector(vec, QUERY_BIAS)).astype(BF16)
    k[...] = dot(normed[...], weight[:, width : 2 * width]).astype(BF16)
    v[...] = (dot(normed[...], weight[:, 2 * width :]) + vector(vec, VALUE_BIAS)).astype(BF16)


def half_lanes(dims, which):
    lane = lax.broadcasted_iota(jnp.int32, dims, len(dims) - 1)
    return (lane < HEAD_WIDTH) == (which == 0)


def attend_forward_kernel(
    tiles, q_ref, own_k, own_v, other_k, other_v, qa_ref, ka_ref, live_ref, o_ref, lse_ref
):
    pair = pl.program_id(0)
    rows = q_ref.shape[0]
    row_tile = rows // tiles
    keys = jnp.concatenate([own_k[...], other_k[...]], axis=0)
    keys = jnp.concatenate([keys, ka_ref[...]], axis=1)
    values = jnp.concatenate([own_v[...], other_v[...]], axis=0)
    lane = lax.broadcasted_iota(jnp.int32, (row_tile, LANES), 1)
    for start in range(0, rows, row_tile):
        here = pl.ds(start, row_tile)
        scaled = q_ref[here, :] * jnp.asarray(HEAD_WIDTH**-0.5, BF16)
        marks = qa_ref[here, :]
        halves, lses = [], []
        for which in range(2):
            own = jnp.where(half_lanes(scaled.shape, which), scaled, jnp.zeros_like(scaled))
            scores = cols_of(jnp.concatenate([own, marks], axis=1), keys)
            peak = jnp.max(scores, axis=1, keepdims=True)
            weights = jnp.exp(scores - peak)
            total = jnp.sum(weights, axis=1, keepdims=True)
            halves.append(dot(weights.astype(BF16), values) / total)
            lses.append(peak + jnp.log(total))
        mixed = jnp.where(lane < HEAD_WIDTH, halves[0], halves[1])
        o_ref[here, :] = (mixed * live_ref[here, :]).astype(BF16)
        kept = jnp.where(pair == 0, jnp.zeros((row_tile, LANES), F32), lse_ref[here, :])
        kept = jnp.where(lane == 2 * pair, lses[0], kept)
        lse_ref[here, :] = jnp.where(lane == 2 * pair + 1, lses[1], kept)


def row_tiles(rows):
    return 1 if rows <= ROW_TILE else rows // 256


def attention_specs(rows, first):
    per_pair = pl.BlockSpec((rows, LANES), lambda i: (0, i + first))
    two = pl.BlockSpec((2, rows, LANES), lambda i: (0, 0, i + first))
    whole = lambda n: pl.BlockSpec((n, LANES), lambda i: (0, 0))
    return per_pair, two, whole(rows), whole(2 * rows)


def ignoring(kernel, start, count):
    return lambda *refs: kernel(*refs[:start], *refs[start + count :])


def attend_forward(first, pairs_here, q, own_k, own_v, other_k, other_v, q_marks, k_marks, live, after=()):
    rows = q.shape[0]
    per_pair, _, marks, all_marks = attention_specs(rows, first)
    out_pair = attention_specs(rows, 0)[0]
    return pl.pallas_call(
        ignoring(partial(attend_forward_kernel, row_tiles(rows)), 8, len(after)),
        grid=(pairs_here,),
        in_specs=[per_pair] * 5 + [marks, all_marks, marks] + [ANY] * len(after),
        out_specs=[out_pair, marks],
        out_shape=[shape((rows, pairs_here * LANES)), shape((rows, LANES), F32)],
        compiler_params=pltpu.CompilerParams(vmem_limit_bytes=(16 if rows <= ROW_TILE else 48) * MIB),
    )(q, own_k, own_v, other_k, other_v, q_marks, k_marks, live, *after)


def widen_kernel(count, tile, *refs):
    attended_parts, refs = refs[:count], refs[count:]
    x_rows, vec, up_shift, own_out, own_up = refs[:5]
    pieces = refs[5:9]
    attended, branch, middle, normed, active, slope, out_weight, up_weight, out_sems, up_sems = refs[9:]
    out_cols = own_out.shape[1]
    out_copies = stage(out_weight, own_out, pieces, 0, 0, out_sems)
    up_copies = stage(up_weight, own_up, pieces, out_cols, 0, up_sems)
    at = 0
    for part in attended_parts:
        attended[:, at : at + part.shape[1]] = part[...]
        at += part.shape[1]
    wait_all(out_copies)
    rows, width = attended.shape
    for start in range(0, rows, tile):
        here = slice(start, start + tile)
        found = dot(attended[here, :], out_weight[...]) + vector(vec, OUT_BIAS)
        branch[here, :] = found
        mid = x_rows[here, :].astype(F32) + vector(vec, SCALE_ATTN) * found
        middle[here, :] = mid
        xhat, _ = norm_parts(mid)
        normed[here, :] = (xhat * vector(vec, LN2_GAIN) + vector(vec, LN2_BIAS)).astype(BF16)
    wait_all(up_copies)

    def widen(block, _):
        cols = pl.ds(pl.multiple_of(block * width, width), width)
        for start in range(0, rows, tile):
            here = slice(start, start + tile)
            hidden = dot(normed[here, :], up_weight[:, cols]) + up_shift[:, cols]
            bell = jnp.exp(-0.5 * hidden * hidden) * (1 / sqrt(2 * pi))
            below = 0.5 + 0.5 * lax.erf(hidden * sqrt(0.5))
            active[here, cols] = (hidden * below).astype(BF16)
            slope[here, cols] = (below + hidden * bell).astype(BF16)
        return 0

    lax.fori_loop(0, up_weight.shape[1] // width, widen, 0)


def down_terms_kernel(chips, *refs):
    active, vec, cots = refs[0], refs[1], refs[2 : 2 + chips]
    cot_rows, down_in, sums = refs[2 + chips : 5 + chips]
    terms = refs[5 + chips :]
    capacity = cots[0].shape[0]
    bias_sum = None
    for i, part in enumerate(cots):
        here = slice(i * capacity, (i + 1) * capacity)
        cot_rows[here, :] = part[...]
        scaled = (part[...].astype(F32) * vector(vec, SCALE_MLP)).astype(BF16)
        down_in[here, :] = scaled
        term = jnp.sum(scaled.astype(F32), axis=0, keepdims=True)
        bias_sum = term if i == 0 else bias_sum + term
    sums[...] = bias_sum
    emit_terms(active, down_in, None, terms, 0)


def down_kernel(chips, tile, *refs):
    active, slope, middle, cot_rows, down_in, vec, own = refs[:7]
    pieces, refs = refs[7:11], refs[11:]
    outs, refs = refs[:chips], refs[chips:]
    hidden_grad, sums, up_shift_grad, weight, sems = refs
    copies = stage(weight, own, pieces, 0, 0, sems)
    rows, width = middle.shape
    capacity = outs[0].shape[0]
    wait_all(copies)
    scale_sum = None
    for i in range(chips):
        here = slice(i * capacity, (i + 1) * capacity)
        found = dot(active[here, :], weight[...]) + vector(vec, DOWN_BIAS)
        outs[i][...] = (middle[here, :] + vector(vec, SCALE_MLP) * found).astype(BF16)
        term = jnp.sum(cot_rows[here, :].astype(F32) * found, axis=0, keepdims=True)
        scale_sum = term if i == 0 else scale_sum + term
    sums[...] = scale_sum

    def back(block, _):
        cols = pl.ds(pl.multiple_of(block * width, width), width)
        total = None
        for start in range(0, rows, tile):
            here = slice(start, start + tile)
            grad = cols_of(down_in[here, :], weight[cols, :])
            grad = (grad * slope[here, cols].astype(F32)).astype(BF16)
            hidden_grad[here, cols] = grad
            term = jnp.sum(grad.astype(F32), axis=0, keepdims=True)
            total = term if start == 0 else total + term
        up_shift_grad[:, cols] = total
        return 0

    lax.fori_loop(0, hidden_grad.shape[1] // width, back, 0)


def narrow_kernel(tile, *refs):
    hidden_grad, middle, branch, vec, own_out, own_up = refs[:6]
    pieces, cot_rows, refs = refs[6:10], refs[10], refs[11:]
    middle_grad, branch_grad, attended_grad, sums = refs[:4]
    out_weight, up_weight, out_sems, up_sems = refs[4:]
    out_cols = own_out.shape[1]
    up_copies = stage(up_weight, own_up, pieces, out_cols, 0, up_sems)
    out_copies = stage(out_weight, own_out, pieces, 0, 0, out_sems)
    wait_all(up_copies)
    rows = middle.shape[0]
    totals = [None] * 4
    for start in range(0, rows, tile):
        here = slice(start, start + tile)
        grad = cols_of(hidden_grad[here, :], up_weight[...])
        xhat, rstd = norm_parts(middle[here, :])
        mid = cot_rows[here, :].astype(F32) + norm_back(grad * vector(vec, LN2_GAIN), xhat, rstd)
        middle_grad[here, :] = mid
        back = (mid * vector(vec, SCALE_ATTN)).astype(BF16)
        branch_grad[here, :] = back
        for i, term in enumerate((grad * xhat, grad, mid * branch[here, :], back.astype(F32))):
            term = jnp.sum(term, axis=0, keepdims=True)
            totals[i] = term if start == 0 else totals[i] + term
    for i, total in enumerate(totals):
        sums[i : i + 1, :] = total
    wait_all(out_copies)
    for start in range(0, rows, tile):
        here = slice(start, start + tile)
        attended_grad[here, :] = cols_of(branch_grad[here, :], out_weight[...]).astype(BF16)


def up_terms_kernel(hidden_grad, normed, branch_grad, attended, *refs):
    terms, (up_scratch, out_scratch) = refs[:8], refs[8:]
    emit_terms(normed, hidden_grad, up_scratch, terms, 0)
    emit_terms(attended, branch_grad, out_scratch, terms, hidden_grad.shape[1])


def attend_backward_kernel(
    tiles,
    skipped,
    q_ref,
    own_k,
    own_v,
    other_k,
    other_v,
    qa_ref,
    ka_ref,
    live_ref,
    o_ref,
    lse_ref,
    g_ref,
    dq_ref,
    own_grad_ref,
    other_grad_ref,
    dk_sum,
    dv_sum,
):
    pair = pl.program_id(0) + skipped
    rows = q_ref.shape[0]
    row_tile = rows // tiles
    key_rows = jnp.concatenate([own_k[...], other_k[...]], axis=0)
    keys = jnp.concatenate([key_rows, ka_ref[...]], axis=1)
    values = jnp.concatenate([own_v[...], other_v[...]], axis=0)
    lane = lax.broadcasted_iota(jnp.int32, (row_tile, LANES), 1)
    scale = HEAD_WIDTH**-0.5
    for start in range(0, rows, row_tile):
        here = pl.ds(start, row_tile)
        scaled = q_ref[here, :] * jnp.asarray(scale, BF16)
        marks = qa_ref[here, :]
        grads = (g_ref[here, :] * live_ref[here, :]).astype(BF16)
        both = grads.astype(F32) * o_ref[here, :].astype(F32)
        halves = []
        key_part = value_part = None
        for which in range(2):
            mine = half_lanes(scaled.shape, which)
            own = jnp.where(mine, scaled, jnp.zeros_like(scaled))
            own_grads = jnp.where(mine, grads, jnp.zeros_like(grads))
            row_dot = jnp.sum(jnp.where(mine, both, 0.0), axis=1, keepdims=True)
            lse = jnp.sum(
                jnp.where(lane == 2 * pair + which, lse_ref[here, :], 0.0), axis=1, keepdims=True
            )
            scores = cols_of(jnp.concatenate([own, marks], axis=1), keys)
            probs = jnp.exp(scores - lse)
            prob_grads = cols_of(own_grads, values)
            score_grads = (probs * (prob_grads - row_dot)).astype(BF16)
            halves.append(dot(score_grads, key_rows))
            value_term = rows_of(probs.astype(BF16), own_grads)
            key_term = rows_of(score_grads, own)
            value_part = value_term if which == 0 else value_part + value_term
            key_part = key_term if which == 0 else key_part + key_term
        mixed = jnp.where(lane < HEAD_WIDTH, halves[0], halves[1])
        dq_ref[here, :] = (mixed * scale).astype(BF16)
        if start == 0:
            dk_sum[...] = key_part
            dv_sum[...] = value_part
        else:
            dk_sum[...] += key_part
            dv_sum[...] += value_part
    own_grad_ref[0] = dk_sum[:rows, :].astype(BF16)
    own_grad_ref[1] = dv_sum[:rows, :].astype(BF16)
    other_grad_ref[0] = dk_sum[rows:, :].astype(BF16)
    other_grad_ref[1] = dv_sum[rows:, :].astype(BF16)


def attend_backward(
    first, pairs_here, skipped, q, own_k, own_v, other_k, other_v, q_marks, k_marks, live, attended, lse, grads, after=()
):
    rows = q.shape[0]
    per_pair, _, marks, all_marks = attention_specs(rows, first)
    out_pair, out_two = attention_specs(rows, 0)[:2]
    there = attention_specs(rows, skipped)[0]
    return pl.pallas_call(
        ignoring(partial(attend_backward_kernel, row_tiles(rows), skipped), 11, len(after)),
        grid=(pairs_here,),
        in_specs=[per_pair] * 5 + [marks, all_marks, marks, there, marks, per_pair]
        + [ANY] * len(after),
        out_specs=[out_pair, out_two, out_two],
        out_shape=[shape((rows, pairs_here * LANES))]
        + [shape((2, rows, pairs_here * LANES))] * 2,
        scratch_shapes=[pltpu.VMEM((2 * rows, LANES), F32)] * 2,
        compiler_params=pltpu.CompilerParams(vmem_limit_bytes=(16 if rows <= ROW_TILE else 48) * MIB),
    )(q, own_k, own_v, other_k, other_v, q_marks, k_marks, live, attended, lse, grads, *after)


def emit_terms(left, right, scratch, terms, at):
    mine, core = lax.axis_index("fsdp"), lax.axis_index("seq") % 2
    count, cols = left.shape[1] // 4, right.shape[1]
    half = count // 2
    here = slice(at, at + cols)
    if scratch is not None:
        scratch[...] = rows_of(left[...], right[...])
    for i in range(2):
        home = core ^ i
        for out, flip in zip(terms[4 * i : 4 * i + 4], (3, 2 - home, 1 + home, 0)):
            start = (mine ^ flip) * count + home * half
            if scratch is not None:
                value = scratch[pl.ds(pl.multiple_of(start, 16), half), :]
            else:
                value = rows_of(left[:, pl.ds(pl.multiple_of(start, LANES), half)], right[...])
            out[:, here] = value.astype(BF16)


def term_shapes(rows, cols):
    return [shape((rows // 2, cols))] * 8


class Reduction:
    def __init__(self, terms):
        self.keep_far, self.keep_side, self.keep_near, self.keep_own = terms[:4]
        self.away = terms[4:]
        self.count = self.keep_far.shape[0]

    def send_other(self):
        self.other_far, self.other_side, self.other_near, self.other_own = [
            to_core(item) for item in self.away
        ]
        return [self.other_far, self.other_side, self.other_near, self.other_own]

    def send_far(self):
        self.far = to_fsdp((wide(self.keep_far) + wide(self.other_far)).astype(BF16), (2, 1))
        return [self.far]

    def send_side(self):
        self.side = to_fsdp((wide(self.keep_side) + wide(self.other_side)).astype(BF16), (2, 1))
        return [self.side]

    def send_near(self):
        total = wide(self.keep_near) + wide(self.other_near) + wide(self.far)
        self.near = to_fsdp(total.astype(BF16), (1, 2))
        return [self.near]

    def send_chips(self):
        flips = [1 << i for i in range((lax.axis_size("seq") // 2).bit_length() - 1)]
        self.orders = list(zip(flips, flips[::-1]))
        total = wide(self.keep_own) + wide(self.other_own)
        self.sent = (total + wide(self.near) + wide(self.side)).astype(BF16)
        self.got = to_chip(self.sent, *self.orders[0])
        return [self.got]

    def send_chips_again(self):
        for order in self.orders[1:]:
            self.sent = (wide(self.sent) + wide(self.got)).astype(BF16)
            self.got = to_chip(self.sent, *order)
        return [self.got]

    def send_total(self):
        self.total = (wide(self.sent) + wide(self.got)).astype(BF16)
        self.other_total = to_core(self.total)
        return [self.other_total]

    def shards(self, widths, after=()):
        outs = [shape((2 * self.count, cols), F32) for cols in widths]
        operands = [(self.total, VMEM), (self.other_total, VMEM)]
        return call(spread_kernel, operands, outs, after=after)


def spread_kernel(own_ref, other_ref, *outs):
    core = lax.axis_index("seq") % 2
    half = own_ref.shape[0]
    at = 0
    for out in outs:
        cols = out.shape[1]
        for i, source in enumerate((own_ref, other_ref)):
            start = pl.multiple_of((core ^ i) * half, 16)
            out[pl.ds(start, half), :] = source[:, at : at + cols].astype(F32)
        at += cols


def project_grad_kernel(count, *refs):
    q_grads, own_grads, other_grads = refs[:count], refs[count : 2 * count], refs[2 * count : 3 * count]
    normed, projected_grad, sums = refs[3 * count : 3 * count + 3]
    terms, scratch = refs[3 * count + 3 : 3 * count + 11], refs[3 * count + 11]
    width = normed.shape[1]
    at = 0
    for q_grad, own_grad, other_grad in zip(q_grads, own_grads, other_grads):
        here = slice(at, at + q_grad.shape[1])
        projected_grad[:, here] = q_grad[...]
        sums[0:1, here] = jnp.sum(q_grad[...].astype(F32), axis=0, keepdims=True)
        for i in range(2):
            both = (own_grad[i].astype(F32) + other_grad[i].astype(F32)).astype(BF16)
            first = (i + 1) * width + at
            projected_grad[:, first : first + q_grad.shape[1]] = both
        sums[1:2, here] = jnp.sum(both.astype(F32), axis=0, keepdims=True)
        at += q_grad.shape[1]
    emit_terms(normed, projected_grad, scratch, terms, 0)


def input_kernel(chips, *refs):
    projected_grad, x_rows, middle_grad, vec = refs[:4]
    qkv_sums, narrow_sums, down_shift_grad, scale_grad, up_shift_grad, own = refs[4:10]
    pieces, rest = refs[10:14], refs[14:]
    outs, sums, weight, sems = rest[:chips], rest[chips], rest[chips + 1], rest[chips + 2]
    copies = stage(weight, own, pieces, 0, EXTRA_ROWS, sems)
    capacity, width = outs[0].shape
    wait_all(copies)
    totals = [None] * 2
    for i in range(chips):
        here = slice(i * capacity, (i + 1) * capacity)
        grad = cols_of(projected_grad[here, :], weight[...])
        xhat, rstd = norm_parts(x_rows[here, :].astype(F32))
        back = norm_back(grad * vector(vec, LN1_GAIN), xhat, rstd)
        outs[i][...] = (middle_grad[here, :] + back).astype(BF16)
        for j, term in enumerate((grad * xhat, grad)):
            term = jnp.sum(term, axis=0, keepdims=True)
            totals[j] = term if i == 0 else totals[j] + term
    sums[...] = jnp.zeros_like(sums)
    for row, value in (
        (LN1_GAIN, totals[0]),
        (LN1_BIAS, totals[1]),
        (QUERY_BIAS, qkv_sums[0:1, :]),
        (VALUE_BIAS, qkv_sums[1:2, :]),
        (OUT_BIAS, narrow_sums[3:4, :]),
        (SCALE_ATTN, narrow_sums[2:3, :]),
        (LN2_GAIN, narrow_sums[0:1, :]),
        (LN2_BIAS, narrow_sums[1:2, :]),
        (DOWN_BIAS, down_shift_grad[...]),
        (SCALE_MLP, scale_grad[...]),
    ):
        sums[row : row + 1, :] = value
    for f in range(4):
        sums[UP_ROW + f : UP_ROW + f + 1, :] = up_shift_grad[:, f * width : (f + 1) * width]


def body(
    tokens,
    image_tokens,
    ln1_gain,
    ln1_bias,
    qkv_weight,
    query_bias,
    value_bias,
    out_weight,
    out_bias,
    scale_attn,
    ln2_gain,
    ln2_bias,
    up_weight,
    up_bias,
    down_weight,
    down_bias,
    scale_mlp,
    cotangent,
):
    seq_count = lax.axis_size("seq")
    fsdp_index = lax.axis_index("fsdp")
    chips = seq_count // 2
    micro_count, tok_count, width = tokens.shape[0], tokens.shape[2], tokens.shape[4]
    slots, images = image_tokens.shape[2:]
    assert chips == micro_count * slots and lax.axis_size("fsdp") == 4
    assert slots * images < PAD_SEGMENT
    capacity = ceil_to((LONG - 2) // seq_count + 2, 16)
    rows = chips * capacity
    tile = rows // 2
    hidden_width = up_weight.shape[1]
    sizes = (slots, images, chips, capacity, tok_count, seq_count)
    counts = image_tokens

    def pick(values, limit=16, after=()):
        return list(
            call(
                partial(pick_kernel, sizes),
                [(counts, SMEM), (values.reshape(micro_count * tok_count, width), VMEM)],
                [shape((capacity, width))] * chips,
                after=after,
                limit=limit,
            )
        )

    def line_up(groups, small=(), limit=16, after=()):
        shards = [shard for group in groups for shard in group]
        more = EXTRA_ROWS if small else 0
        outs = [
            shape((group[0].shape[0] + more, sum(shard.shape[1] for shard in group)))
            for group in groups
        ]
        if small:
            outs += [shape(((outs[0].shape[0] + more) // 2, outs[0].shape[1]))]
        return call(
            partial(line_up_kernel, [len(group) for group in groups], len(small)),
            [(item, VMEM) for item in shards + list(small)],
            outs,
            [pltpu.VMEM((EXTRA_ROWS, width), F32)] if small else [],
            after=after,
            limit=limit,
        )

    def cross(parts, bit):
        labels = [label for label in range(chips) if label & bit]
        return to_chip(jnp.concatenate([parts[label] for label in labels]), *flips_of(bit, chips))

    def crossed(parts, moved, bit):
        parts = list(parts)
        for i, label in enumerate(label for label in range(chips) if label & bit):
            parts[label] = moved[i * capacity : (i + 1) * capacity]
        return parts

    def cross_rest(parts):
        bit = 2
        while 2 * bit < chips:
            parts = crossed(parts, cross(parts, bit), bit)
            bit *= 2
        return parts, cross(parts, bit), bit

    def collect(parts, after=()):
        return call(
            partial(collect_kernel, sizes),
            [(counts, SMEM)] + [(part, VMEM) for part in parts],
            [shape((micro_count * tok_count, width))],
            after=after,
        )[0]

    small = [
        ln1_gain,
        ln1_bias,
        query_bias,
        value_bias,
        out_bias,
        scale_attn,
        ln2_gain,
        ln2_bias,
        down_bias,
        scale_mlp,
    ]
    own_rows = ln1_gain.shape[0]
    qkv_sent, qkv_first = line_up([[qkv_weight]], small + [up_bias], limit=60)
    near, far = to_fsdp(qkv_sent, (1, 2)), to_fsdp(qkv_first, (3, 3))
    x_parts = pick(tokens, limit=60, after=[qkv_sent])
    for label in range(chips - 1, 0, -1):
        x_parts[label] = to_chip(x_parts[label], *flips_of(label, chips))
    cot_sent = pick(cotangent, after=[qkv_sent])
    up_sent, down_sent = line_up([[out_weight, up_weight], [down_weight]], after=[qkv_sent])
    q_marks, k_marks, live = call(
        partial(marks_kernel, sizes),
        [(counts, SMEM)],
        [shape((rows, LANES)), shape((2 * rows, LANES)), shape((rows, LANES), F32)],
        after=[qkv_sent],
    )
    near, far, up_sent = hold([near, far, up_sent], x_parts + [q_marks, down_sent, cot_sent[0]])
    qkv_pieces = [near, to_core(near), far, to_core(far)]
    up_near = to_fsdp(up_sent, (1, 2))

    x_rows, normed_first, q, own_k, own_v, vec, up_shift = call(
        partial(project_kernel, chips),
        [(part, VMEM) for part in x_parts]
        + [(item, ANY) for item in [qkv_sent, qkv_weight] + qkv_pieces],
        [shape((rows, width))] * 5
        + [shape((EXTRA_ROWS, width), F32), shape((1, hidden_width), F32)],
        [
            pltpu.VMEM((width, 3 * width), BF16),
            pltpu.VMEM((4, EXTRA_ROWS, width), BF16),
            STAGE_SEMS,
            pltpu.SemaphoreType.DMA((4,)),
        ],
    )
    down_sent, *cot_sent = hold([down_sent] + cot_sent, [q])
    down_near = to_fsdp(down_sent, (1, 2))
    cot_moved = cross(cot_sent, 1)
    attention = (q, own_k, own_v, to_core(own_k), to_core(own_v), q_marks, k_marks, live)
    spans = [(0, 2), (2, width // LANES - 2)]
    attended_parts, lses = [], []

    def forward(i):
        part, lse = attend_forward(*spans[i], *attention, after=attended_parts[-1:])
        attended_parts.append(part)
        lses.append(lse)
        return part

    up_near, cot_moved = hold([up_near, cot_moved], [forward(0)])
    cot_parts = crossed(cot_sent, cot_moved, 1)
    up_far = to_fsdp(up_near[: own_rows // 2], (2, 1))
    cot_parts, cot_moved, last_bit = cross_rest(cot_parts)
    up_far, down_near, cot_moved = hold([up_far, down_near, cot_moved], [forward(1)])
    cot_parts = crossed(cot_parts, cot_moved, last_bit)
    up_pieces = [up_near, to_core(up_near), up_far, to_core(up_far)]
    down_far = to_fsdp(down_near[: down_weight.shape[0] // 2], (2, 1))
    up_pieces = hold(up_pieces, [])
    (down_near,) = hold([down_near], up_pieces)
    down_other = to_core(down_near)

    up_scratch = [
        pltpu.VMEM((width, width), BF16),
        pltpu.VMEM((width, hidden_width), BF16),
        STAGE_SEMS,
        STAGE_SEMS,
    ]
    attended, branch, middle, normed_second, active, slope = call(
        partial(widen_kernel, len(attended_parts), tile),
        [(item, VMEM) for item in attended_parts + [x_rows, vec, up_shift]]
        + [(item, ANY) for item in [out_weight, up_weight] + up_pieces],
        [
            shape((rows, width)),
            shape((rows, width), F32),
            shape((rows, width), F32),
            shape((rows, width)),
            shape((rows, hidden_width)),
            shape((rows, hidden_width)),
        ],
        up_scratch,
    )
    down_far, down_other = hold([down_far, down_other], [attended])
    far_other = to_core(down_far)
    cot_rows, down_in, down_shift_grad, *down_terms = call(
        partial(down_terms_kernel, chips),
        [(item, VMEM) for item in [active, vec] + cot_parts],
        [shape((rows, width)), shape((rows, width)), shape((1, width), F32)]
        + term_shapes(down_weight.shape[0], width),
        after=[down_far],
    )
    down = Reduction(down_terms)
    down_pieces = [down_near, down_other, down_far, far_other]
    *down.away, down_near, down_other, down_far, far_other = hold(
        list(down.away) + down_pieces, [down_in]
    )
    down_pieces = [down_near, down_other, down_far, far_other]
    others = down.send_other()
    (down.other_far,) = hold(others[:1], [])
    waits = down.send_far() + others[1:]
    results = call(
        partial(down_kernel, chips, tile),
        [(item, VMEM) for item in (active, slope, middle, cot_rows, down_in, vec)]
        + [(item, ANY) for item in [down_weight] + down_pieces],
        [shape((capacity, width))] * chips
        + [
            shape((rows, hidden_width)),
            shape((1, width), F32),
            shape((1, hidden_width), F32),
        ],
        [pltpu.VMEM((hidden_width, width), BF16), STAGE_SEMS],
    )
    out_sent, (hidden_grad, scale_grad, up_shift_grad) = list(results[:chips]), results[chips:]
    down.far, down.other_side, down.other_near, down.other_own = hold(waits, [hidden_grad])
    waits = down.send_near() + down.send_side()
    out_moved = cross(out_sent, 1)

    middle_grad, branch_grad, attended_grad, narrow_sums = call(
        partial(narrow_kernel, tile),
        [(item, VMEM) for item in (hidden_grad, middle, branch, vec)]
        + [(item, ANY) for item in [out_weight, up_weight] + up_pieces]
        + [(cot_rows, VMEM)],
        [
            shape((rows, width), F32),
            shape((rows, width)),
            shape((rows, width)),
            shape((4, width), F32),
        ],
        up_scratch,
    )
    up_terms = call(
        up_terms_kernel,
        [(item, VMEM) for item in (hidden_grad, normed_second, branch_grad, attended)],
        term_shapes(own_rows, hidden_width + width),
        [pltpu.VMEM((width, hidden_width), F32), pltpu.VMEM((width, width), F32)],
    )
    up = Reduction(up_terms)

    query_grads, own_grads, other_grads = [], [], []

    def backward(first, after=()):
        query_grad, own_grad, other_grad = attend_backward(
            first,
            1,
            first - spans[first >= spans[1][0]][0],
            *attention,
            attended_parts[first >= spans[1][0]],
            lses[first >= spans[1][0]],
            attended_grad,
            after=query_grads[-1:] + list(after),
        )
        query_grads.append(query_grad)
        own_grads.append(own_grad)
        other_grads.append(other_grad)
        return query_grad

    def hold_grads(arrays):
        first, count = sent_grads[0], len(arrays)
        items = hold(list(arrays) + other_grads[first:], query_grads[-1:])
        other_grads[first:] = items[count:]
        sent_grads[0] = len(other_grads)
        return items[:count], [to_core(item) for item in other_grads[first:]]

    sent_grads = [0]
    core_grads = []

    down.near, down.side, out_moved, *up.away = hold(
        waits + [out_moved] + list(up.away), up_terms[:1]
    )
    others = up.send_other()
    waits = down.send_chips()
    up.other_far, up.other_side = hold(others[:2], [])
    waits += up.send_far() + up.send_side() + others[2:]
    backward(0)
    backward(1)
    (down.got, up.far, up.side, up.other_near, up.other_own), fresh = hold_grads(waits)
    waits = up.send_near() + down.send_chips_again() + fresh
    backward(2)
    backward(3)
    (up.near, down.got, *core_grads), fresh = hold_grads(waits)
    waits = up.send_chips() + down.send_total() + fresh
    backward(4)
    backward(5)
    (down.other_total, *more), fresh = hold_grads(waits[1:])
    core_grads += more + fresh
    (down_grad,) = down.shards([width])
    out_parts, out_moved, _ = cross_rest(crossed(out_sent, out_moved, 1))

    projected_grad, qkv_sums, *qkv_terms = call(
        partial(project_grad_kernel, len(query_grads)),
        [(item, VMEM) for item in query_grads + own_grads + core_grads + [normed_first]],
        [shape((rows, 3 * width)), shape((2, width), F32)] + term_shapes(own_rows, 3 * width),
        [pltpu.VMEM((width, 3 * width), F32)],
        after=[down_grad],
    )
    qkv = Reduction(qkv_terms)
    *qkv.away, up.got = hold(list(qkv.away) + waits[:1], [projected_grad])
    up_waits = up.send_chips_again()
    others = qkv.send_other()
    qkv.other_far, qkv.other_side = hold(others[:2], [])
    waits = qkv.send_far() + qkv.send_side() + others[2:]
    *in_sent, sums = call(
        partial(input_kernel, chips),
        [(item, VMEM) for item in (projected_grad, x_rows, middle_grad, vec)]
        + [(item, VMEM) for item in (qkv_sums, narrow_sums, down_shift_grad, scale_grad, up_shift_grad)]
        + [(item, ANY) for item in [qkv_weight] + qkv_pieces],
        [shape((capacity, width))] * chips + [shape((EXTRA_ROWS, width), F32)],
        [pltpu.VMEM((width, 3 * width), BF16), STAGE_SEMS],
    )
    qkv.far, qkv.side, qkv.other_near, qkv.other_own, sums, *in_sent = hold(
        waits + [sums] + in_sent, []
    )
    waits = qkv.send_near()
    in_moved = cross(in_sent, 1)
    other_sums = to_core(sums)
    qkv.near, in_moved, up.got, out_moved, sums, other_sums = hold(
        waits + [in_moved] + up_waits + [out_moved, sums, other_sums], []
    )
    out_parts = crossed(out_parts, out_moved, last_bit)
    up.send_total()
    waits = qkv.send_chips()
    in_parts, in_moved, _ = cross_rest(crossed(in_sent, in_moved, 1))
    sums = sums + other_sums
    far_sums = [to_chip(sums, flip) for flip in (1, 2, 3)]
    output = collect(out_parts)
    (up.other_total,) = hold([up.other_total], [output])
    up_grad, out_grad = up.shards([hidden_width, width])
    qkv.got, sums, in_moved, *far_sums = hold(waits + [sums, in_moved] + far_sums, [up_grad])
    waits = qkv.send_chips_again()
    sums = (sums + far_sums[0]) + (far_sums[1] + far_sums[2])
    flip = 4
    while flip < chips:
        sums = sums + to_chip(sums, flip)
        flip *= 2
    far_sums = [to_fsdp(sums, (flip, flip)) for flip in (1, 2, 3)]
    input_grad = collect(crossed(in_parts, in_moved, last_bit))
    qkv.got, sums, *far_sums = hold(waits + [sums] + far_sums, [input_grad])
    sums = (sums + far_sums[0]) + (far_sums[1] + far_sums[2])
    qkv.send_total()
    (qkv_grad,) = qkv.shards([3 * width])
    output, input_grad = output.reshape(tokens.shape), input_grad.reshape(tokens.shape)

    small_grads = lax.dynamic_slice_in_dim(sums[:UP_ROW], fsdp_index * own_rows, own_rows, 1)
    up_shift_total = lax.dynamic_index_in_dim(sums, UP_ROW + fsdp_index, 0, keepdims=False)
    return (
        output,
        input_grad,
        small_grads[LN1_GAIN],
        small_grads[LN1_BIAS],
        qkv_grad,
        small_grads[QUERY_BIAS],
        small_grads[VALUE_BIAS],
        out_grad,
        small_grads[OUT_BIAS],
        small_grads[SCALE_ATTN],
        small_grads[LN2_GAIN],
        small_grads[LN2_BIAS],
        up_grad,
        up_shift_total,
        down_grad,
        small_grads[DOWN_BIAS],
        small_grads[SCALE_MLP],
    )


def solution(mesh):
    vector, matrix = P("fsdp"), P("fsdp", None)
    places = P(None, "fsdp", None, "seq", None)
    return jax.shard_map(
        body,
        mesh=mesh,
        in_specs=(
            places,
            P(None, "fsdp", None, None),
            vector,
            vector,
            matrix,
            vector,
            vector,
            matrix,
            vector,
            vector,
            vector,
            vector,
            matrix,
            vector,
            matrix,
            vector,
            vector,
            places,
        ),
        out_specs=(
            places,
            places,
            vector,
            vector,
            matrix,
            vector,
            vector,
            matrix,
            vector,
            vector,
            vector,
            vector,
            matrix,
            vector,
            matrix,
            vector,
            vector,
        ),
        check_vma=False,
    )
```

```python
from functools import partial
from math import pi, sqrt

import jax
import jax.numpy as jnp
from jax import lax
from jax.experimental import pallas as pl
from jax.experimental.pallas import tpu as pltpu
from jax.sharding import PartitionSpec as P

LONG = 1029
EPSILON = 1e-06
MASK_VALUE = -1e30
PAD_SEGMENT = 127
LANES = 128
HEAD_WIDTH = 64
MIB = 2**20
BOTH = ("fsdp", "seq")
F32 = jnp.float32
BF16 = jnp.bfloat16
VMEM = pl.BlockSpec()
SMEM = pl.BlockSpec(memory_space=pltpu.SMEM)
ANY = pl.BlockSpec(memory_space=pl.ANY)

LN1_GAIN, LN1_BIAS, QUERY_BIAS, VALUE_BIAS, OUT_BIAS = 0, 1, 2, 3, 4
SCALE_ATTN, LN2_GAIN, LN2_BIAS, DOWN_BIAS, SCALE_MLP, UP_ROW = 5, 6, 7, 8, 9, 10


def ceil_to(value, step):
    return (value + step - 1) // step * step


def move(value, flips):
    fsdp_count, seq_count = lax.axis_size("fsdp"), lax.axis_size("seq")
    pairs = []
    for f in range(fsdp_count):
        for s in range(seq_count):
            fsdp_flip, chip_flip, core_flip = flips[s % 2]
            there = (f ^ fsdp_flip) * seq_count + (s ^ (2 * chip_flip + core_flip))
            pairs.append((f * seq_count + s, there))
    return lax.ppermute(value, BOTH, pairs)


def to_core(value):
    return move(value, [(0, 0, 1)] * 2)


def to_chip(value, flip, other_flip=None):
    return move(value, [(0, flip, 0), (0, flip if other_flip is None else other_flip, 0)])


def to_fsdp(value, flips):
    return move(value, [(flip, 0, 0) for flip in flips])


def wide(value):
    return value.astype(F32)


def dot(left, right):
    return jnp.dot(left, right, preferred_element_type=F32)


def rows_of(left, right):
    return lax.dot_general(left, right, (((0,), (0,)), ((), ())), preferred_element_type=F32)


def cols_of(left, right):
    return lax.dot_general(left, right, (((1,), (1,)), ((), ())), preferred_element_type=F32)


def shape(dims, dtype=BF16):
    return jax.ShapeDtypeStruct(dims, dtype)


def call(kernel, operands, outs, scratch=(), after=(), limit=16, aliases=None):
    count = len(operands)

    def run(*refs):
        kernel(*refs[:count], *refs[count + len(after) :])

    return pl.pallas_call(
        run,
        in_specs=[spec for _, spec in operands] + [ANY] * len(after),
        out_specs=[ANY if aliases else VMEM] * len(outs),
        out_shape=list(outs),
        scratch_shapes=list(scratch),
        input_output_aliases=aliases or {},
        compiler_params=pltpu.CompilerParams(vmem_limit_bytes=limit * MIB),
    )(*[array for array, _ in operands], *after)


def hold(arrays, after):
    results = call(
        lambda *refs: None,
        [(item, ANY) for item in arrays],
        [shape(item.shape, item.dtype) for item in arrays],
        after=after,
        aliases={i: i for i in range(len(arrays))},
    )
    return list(results)


def flips_of(label, chips):
    bits = chips.bit_length() - 1
    return sum(((label >> i) & 1) << (bits - 1 - i) for i in range(bits)), label


def flip_of(label, core, chips):
    first, second = flips_of(label, chips)
    return label if first == second else jnp.where(core == 0, first, second)


def places_of(counts_ref, slots, images, chip, source, tok_count, seq_count):
    micro, slot = chip // slots, chip % slots
    total = jnp.int32(0)
    ends, sizes = [], []
    for j in range(slots):
        size = jnp.int32(0)
        for i in range(images):
            size = size + counts_ref[micro, 0, j, i]
            ends.append(total + size)
        sizes.append(size)
        total = total + size
    free = seq_count * tok_count - total
    start, room_end = jnp.int32(0), jnp.int32(0)
    picked = [jnp.int32(0)] * 4
    for j in range(slots):
        room = LONG - sizes[j]
        span = (
            start,
            start + sizes[j],
            total + jnp.minimum(room_end, free),
            total + jnp.minimum(room_end + room, free),
        )
        picked = [jnp.where(slot == j, a, b) for a, b in zip(span, picked)]
        start, room_end = start + sizes[j], room_end + room
    first, last, more, stop = [(a - source + seq_count - 1) // seq_count for a in picked]
    return micro, first, last - first, more, stop - more, total, ends


def local_rows_of(step, first, count, more, extra):
    local = jnp.where(step < count, first + step, more + step - count)
    return local, step < count + extra


def pick_kernel(sizes, counts_ref, values, *parts):
    slots, images, chips, capacity, tok_count, seq_count = sizes
    seq_index = lax.axis_index("seq")
    chip, core = seq_index // 2, seq_index % 2
    for label in range(chips):
        flip = flip_of(label, core, chips)
        micro, first, count, more, extra, _, _ = places_of(
            counts_ref, slots, images, chip ^ flip, seq_index, tok_count, seq_count
        )
        step = lax.broadcasted_iota(jnp.int32, (capacity, tok_count), 0)
        held = lax.broadcasted_iota(jnp.int32, (capacity, tok_count), 1)
        local, valid = local_rows_of(step, first, count, more, extra)
        pick = jnp.where(valid & (local == held), 1.0, 0.0).astype(BF16)
        start = pl.multiple_of(micro * tok_count, tok_count)
        parts[label][...] = dot(pick, values[pl.ds(start, tok_count), :]).astype(BF16)


def line_up_kernel(groups, small_count, *refs):
    shards, refs = refs[: sum(groups)], refs[sum(groups) :]
    smalls, refs = refs[:small_count], refs[small_count:]
    halves, rest = refs[: len(groups)], refs[len(groups) :]
    core = lax.axis_index("seq") % 2
    if smalls:
        first_half, inserted = rest
        half = (halves[0].shape[0] - EXTRA_ROWS) // 2
        inserted[...] = jnp.zeros_like(inserted)
        for i, small in enumerate(smalls):
            length = small.shape[0]
            inserted[i : i + 1, :length] = small[...].astype(F32).reshape(1, length)
        halves[0][half : half + EXTRA_ROWS, : inserted.shape[1]] = inserted[...].astype(BF16)
    at = 0
    for count, out in zip(groups, halves):
        half = shards[at].shape[0] // 2
        for i in range(2):
            start = pl.multiple_of((core ^ i) * half, 16)
            row = i * (out.shape[0] - half)
            col = 0
            for shard in shards[at : at + count]:
                out[row : row + half, col : col + shard.shape[1]] = shard[pl.ds(start, half), :]
                col += shard.shape[1]
        at += count
    if smalls:
        first_half[...] = halves[0][: first_half.shape[0], :]


def collect_kernel(sizes, counts_ref, *refs):
    slots, images, chips, capacity, tok_count, seq_count = sizes
    parts, out = refs[:chips], refs[chips]
    seq_index = lax.axis_index("seq")
    micros = chips // slots
    sums = [None] * micros
    for label in range(chips):
        flip = flip_of(label, seq_index % 2, chips)
        micro, first, count, more, extra, _, _ = places_of(
            counts_ref, slots, images, seq_index // 2 ^ flip, seq_index, tok_count, seq_count
        )
        step = lax.broadcasted_iota(jnp.int32, (tok_count, capacity), 1)
        held = lax.broadcasted_iota(jnp.int32, (tok_count, capacity), 0)
        local, valid = local_rows_of(step, first, count, more, extra)
        pick = jnp.where(valid & (local == held), 1.0, 0.0).astype(BF16)
        found = dot(pick, parts[label][...])
        for m in range(micros):
            term = jnp.where(micro == m, found, 0.0)
            sums[m] = term if sums[m] is None else sums[m] + term
    for m in range(micros):
        out[m * tok_count : (m + 1) * tok_count, :] = sums[m].astype(BF16)


def marks_kernel(sizes, counts_ref, q_marks, k_marks, live_ref):
    slots, images, chips, capacity, tok_count, seq_count = sizes
    rows = chips * capacity
    seq_index = lax.axis_index("seq")
    chip, core = seq_index // 2, seq_index % 2
    row = lax.broadcasted_iota(jnp.int32, (rows, LANES), 0)
    lane = lax.broadcasted_iota(jnp.int32, (rows, LANES), 1)
    for which in range(2):
        segment = jnp.full((rows, LANES), PAD_SEGMENT, jnp.int32)
        live = jnp.zeros((rows, LANES), jnp.int32)
        for label in range(chips):
            flip = flip_of(label, core ^ which, chips)
            source = 2 * (chip ^ flip) + (core ^ which)
            _, first, count, more, extra, total, ends = places_of(
                counts_ref, slots, images, chip, source, tok_count, seq_count
            )
            step = row - label * capacity
            local, valid = local_rows_of(step, first, count, more, extra)
            valid = valid & (step >= 0) & (step < capacity)
            place = local * seq_count + source
            image = jnp.zeros((rows, LANES), jnp.int32)
            for end in ends:
                image = image + (end <= place).astype(jnp.int32)
            segment = jnp.where(valid, image, segment)
            live = jnp.where(valid & (place < total), 1, live)
        same = segment == lane
        k_marks[which * rows : (which + 1) * rows, :] = jnp.where(same, 0.0, MASK_VALUE).astype(
            BF16
        )
        if which == 0:
            q_marks[...] = jnp.where(same, 1.0, 0.0).astype(BF16)
            live_ref[...] = live.astype(F32)


def stage(out, own, pieces, first_col, extra, sems):
    rows, cols = own.shape
    half = rows // 2
    mine, core = lax.axis_index("fsdp"), lax.axis_index("seq") % 2
    copies = []

    def put(source, flip, at):
        start = pl.multiple_of((mine ^ flip) * rows + at, 16)
        copy = pltpu.make_async_copy(
            source, out.at[pl.ds(start, source.shape[0])], sems.at[len(copies)]
        )
        copy.start()
        copies.append(copy)

    here = slice(first_col, first_col + cols)
    put(own, 0, 0)
    for i in range(2):
        home = core ^ i
        near, far = pieces[i], pieces[2 + i]
        put(near.at[:half, here], 1 + home, home * half)
        put(near.at[half + extra :, here], 1 + home, (1 - home) * half)
        put(far.at[:half, here], 3, home * half)
    return copies


def wait_all(copies):
    for copy in copies:
        copy.wait()


STAGE_SEMS = pltpu.SemaphoreType.DMA((7,))
EXTRA_ROWS = 16
ROW_TILE = 640


def norm_parts(values):
    center = values - jnp.mean(values, axis=-1, keepdims=True)
    rstd = lax.rsqrt(jnp.mean(center * center, axis=-1, keepdims=True) + EPSILON)
    return center * rstd, rstd


def norm_back(e, xhat, rstd):
    return rstd * (
        e
        - jnp.mean(e, axis=-1, keepdims=True)
        - xhat * jnp.mean(e * xhat, axis=-1, keepdims=True)
    )


def vector(ref, row):
    return ref[row : row + 1, :]


def project_kernel(chips, *refs):
    x_parts, sent, own, pieces = refs[:chips], refs[chips], refs[chips + 1], refs[chips + 2 : chips + 6]
    x_rows, normed, q, k, v, vec, up_shift, weight, vectors, sems, vector_sems = refs[chips + 6 :]
    copies = stage(weight, own, pieces, 0, EXTRA_ROWS, sems)
    capacity, width = x_parts[0].shape
    half = own.shape[0] // 2
    mine, core = lax.axis_index("fsdp"), lax.axis_index("seq") % 2
    vector_copies = []
    for i, (source, flip) in enumerate(
        ((sent, 0), (pieces[0], 1 + core), (pieces[1], 2 - core), (pieces[2], 3))
    ):
        copy = pltpu.make_async_copy(
            source.at[half : half + EXTRA_ROWS, :width], vectors.at[mine ^ flip], vector_sems.at[i]
        )
        copy.start()
        vector_copies.append(copy)
    wait_all(vector_copies)
    shard = width // 4
    vec[...] = jnp.concatenate([wide(vectors[f, :, :shard]) for f in range(4)], axis=1)
    for f in range(4):
        up_shift[:, f * width : (f + 1) * width] = wide(vectors[f])[UP_ROW : UP_ROW + 1, :]
    for i, part in enumerate(x_parts):
        here = slice(i * capacity, (i + 1) * capacity)
        x_rows[here, :] = part[...]
        xhat, _ = norm_parts(part[...].astype(F32))
        normed[here, :] = (xhat * vector(vec, LN1_GAIN) + vector(vec, LN1_BIAS)).astype(BF16)
    wait_all(copies)
    q[...] = (dot(normed[...], weight[:, :width]) + vector(vec, QUERY_BIAS)).astype(BF16)
    k[...] = dot(normed[...], weight[:, width : 2 * width]).astype(BF16)
    v[...] = (dot(normed[...], weight[:, 2 * width :]) + vector(vec, VALUE_BIAS)).astype(BF16)


def half_lanes(dims, which):
    lane = lax.broadcasted_iota(jnp.int32, dims, len(dims) - 1)
    return (lane < HEAD_WIDTH) == (which == 0)


def attend_forward_kernel(
    tiles, q_ref, own_k, own_v, other_k, other_v, qa_ref, ka_ref, live_ref, o_ref, lse_ref
):
    pair = pl.program_id(0)
    rows = q_ref.shape[0]
    row_tile = rows // tiles
    keys = jnp.concatenate([own_k[...], other_k[...]], axis=0)
    keys = jnp.concatenate([keys, ka_ref[...]], axis=1)
    values = jnp.concatenate([own_v[...], other_v[...]], axis=0)
    lane = lax.broadcasted_iota(jnp.int32, (row_tile, LANES), 1)
    for start in range(0, rows, row_tile):
        here = pl.ds(start, row_tile)
        scaled = q_ref[here, :] * jnp.asarray(HEAD_WIDTH**-0.5, BF16)
        marks = qa_ref[here, :]
        halves, lses = [], []
        for which in range(2):
            own = jnp.where(half_lanes(scaled.shape, which), scaled, jnp.zeros_like(scaled))
            scores = cols_of(jnp.concatenate([own, marks], axis=1), keys)
            peak = jnp.max(scores, axis=1, keepdims=True)
            weights = jnp.exp(scores - peak)
            total = jnp.sum(weights, axis=1, keepdims=True)
            halves.append(dot(weights.astype(BF16), values) / total)
            lses.append(peak + jnp.log(total))
        mixed = jnp.where(lane < HEAD_WIDTH, halves[0], halves[1])
        o_ref[here, :] = (mixed * live_ref[here, :]).astype(BF16)
        kept = jnp.where(pair == 0, jnp.zeros((row_tile, LANES), F32), lse_ref[here, :])
        kept = jnp.where(lane == 2 * pair, lses[0], kept)
        lse_ref[here, :] = jnp.where(lane == 2 * pair + 1, lses[1], kept)


def row_tiles(rows):
    return 1 if rows <= ROW_TILE else rows // 256


def attention_specs(rows, first):
    per_pair = pl.BlockSpec((rows, LANES), lambda i: (0, i + first))
    two = pl.BlockSpec((2, rows, LANES), lambda i: (0, 0, i + first))
    whole = lambda n: pl.BlockSpec((n, LANES), lambda i: (0, 0))
    return per_pair, two, whole(rows), whole(2 * rows)


def ignoring(kernel, start, count):
    return lambda *refs: kernel(*refs[:start], *refs[start + count :])


def attend_forward(first, pairs_here, q, own_k, own_v, other_k, other_v, q_marks, k_marks, live, after=()):
    rows = q.shape[0]
    per_pair, _, marks, all_marks = attention_specs(rows, first)
    out_pair = attention_specs(rows, 0)[0]
    return pl.pallas_call(
        ignoring(partial(attend_forward_kernel, row_tiles(rows)), 8, len(after)),
        grid=(pairs_here,),
        in_specs=[per_pair] * 5 + [marks, all_marks, marks] + [ANY] * len(after),
        out_specs=[out_pair, marks],
        out_shape=[shape((rows, pairs_here * LANES)), shape((rows, LANES), F32)],
        compiler_params=pltpu.CompilerParams(vmem_limit_bytes=(16 if rows <= ROW_TILE else 48) * MIB),
    )(q, own_k, own_v, other_k, other_v, q_marks, k_marks, live, *after)


def widen_kernel(count, tile, *refs):
    attended_parts, refs = refs[:count], refs[count:]
    x_rows, vec, up_shift, own_out, own_up = refs[:5]
    pieces = refs[5:9]
    attended, branch, middle, normed, active, slope, out_weight, up_weight, out_sems, up_sems = refs[9:]
    out_cols = own_out.shape[1]
    out_copies = stage(out_weight, own_out, pieces, 0, 0, out_sems)
    up_copies = stage(up_weight, own_up, pieces, out_cols, 0, up_sems)
    at = 0
    for part in attended_parts:
        attended[:, at : at + part.shape[1]] = part[...]
        at += part.shape[1]
    wait_all(out_copies)
    rows, width = attended.shape
    for start in range(0, rows, tile):
        here = slice(start, start + tile)
        found = dot(attended[here, :], out_weight[...]) + vector(vec, OUT_BIAS)
        branch[here, :] = found
        mid = x_rows[here, :].astype(F32) + vector(vec, SCALE_ATTN) * found
        middle[here, :] = mid
        xhat, _ = norm_parts(mid)
        normed[here, :] = (xhat * vector(vec, LN2_GAIN) + vector(vec, LN2_BIAS)).astype(BF16)
    wait_all(up_copies)

    def widen(block, _):
        cols = pl.ds(pl.multiple_of(block * width, width), width)
        for start in range(0, rows, tile):
            here = slice(start, start + tile)
            hidden = dot(normed[here, :], up_weight[:, cols]) + up_shift[:, cols]
            bell = jnp.exp(-0.5 * hidden * hidden) * (1 / sqrt(2 * pi))
            below = 0.5 + 0.5 * lax.erf(hidden * sqrt(0.5))
            active[here, cols] = (hidden * below).astype(BF16)
            slope[here, cols] = (below + hidden * bell).astype(BF16)
        return 0

    lax.fori_loop(0, up_weight.shape[1] // width, widen, 0)


def down_terms_kernel(chips, *refs):
    active, vec, cots = refs[0], refs[1], refs[2 : 2 + chips]
    cot_rows, down_in, sums = refs[2 + chips : 5 + chips]
    terms = refs[5 + chips :]
    capacity = cots[0].shape[0]
    bias_sum = None
    for i, part in enumerate(cots):
        here = slice(i * capacity, (i + 1) * capacity)
        cot_rows[here, :] = part[...]
        scaled = (part[...].astype(F32) * vector(vec, SCALE_MLP)).astype(BF16)
        down_in[here, :] = scaled
        term = jnp.sum(scaled.astype(F32), axis=0, keepdims=True)
        bias_sum = term if i == 0 else bias_sum + term
    sums[...] = bias_sum
    emit_terms(active, down_in, None, terms, 0)


def down_kernel(chips, tile, *refs):
    active, slope, middle, cot_rows, down_in, vec, own = refs[:7]
    pieces, refs = refs[7:11], refs[11:]
    outs, refs = refs[:chips], refs[chips:]
    hidden_grad, sums, up_shift_grad, weight, sems = refs
    copies = stage(weight, own, pieces, 0, 0, sems)
    rows, width = middle.shape
    capacity = outs[0].shape[0]
    wait_all(copies)
    scale_sum = None
    for i in range(chips):
        here = slice(i * capacity, (i + 1) * capacity)
        found = dot(active[here, :], weight[...]) + vector(vec, DOWN_BIAS)
        outs[i][...] = (middle[here, :] + vector(vec, SCALE_MLP) * found).astype(BF16)
        term = jnp.sum(cot_rows[here, :].astype(F32) * found, axis=0, keepdims=True)
        scale_sum = term if i == 0 else scale_sum + term
    sums[...] = scale_sum

    def back(block, _):
        cols = pl.ds(pl.multiple_of(block * width, width), width)
        total = None
        for start in range(0, rows, tile):
            here = slice(start, start + tile)
            grad = cols_of(down_in[here, :], weight[cols, :])
            grad = (grad * slope[here, cols].astype(F32)).astype(BF16)
            hidden_grad[here, cols] = grad
            term = jnp.sum(grad.astype(F32), axis=0, keepdims=True)
            total = term if start == 0 else total + term
        up_shift_grad[:, cols] = total
        return 0

    lax.fori_loop(0, hidden_grad.shape[1] // width, back, 0)


def narrow_kernel(tile, *refs):
    hidden_grad, middle, branch, vec, own_out, own_up = refs[:6]
    pieces, cot_rows, refs = refs[6:10], refs[10], refs[11:]
    middle_grad, branch_grad, attended_grad, sums = refs[:4]
    out_weight, up_weight, out_sems, up_sems = refs[4:]
    out_cols = own_out.shape[1]
    up_copies = stage(up_weight, own_up, pieces, out_cols, 0, up_sems)
    out_copies = stage(out_weight, own_out, pieces, 0, 0, out_sems)
    wait_all(up_copies)
    rows = middle.shape[0]
    totals = [None] * 4
    for start in range(0, rows, tile):
        here = slice(start, start + tile)
        grad = cols_of(hidden_grad[here, :], up_weight[...])
        xhat, rstd = norm_parts(middle[here, :])
        mid = cot_rows[here, :].astype(F32) + norm_back(grad * vector(vec, LN2_GAIN), xhat, rstd)
        middle_grad[here, :] = mid
        back = (mid * vector(vec, SCALE_ATTN)).astype(BF16)
        branch_grad[here, :] = back
        for i, term in enumerate((grad * xhat, grad, mid * branch[here, :], back.astype(F32))):
            term = jnp.sum(term, axis=0, keepdims=True)
            totals[i] = term if start == 0 else totals[i] + term
    for i, total in enumerate(totals):
        sums[i : i + 1, :] = total
    wait_all(out_copies)
    for start in range(0, rows, tile):
        here = slice(start, start + tile)
        attended_grad[here, :] = cols_of(branch_grad[here, :], out_weight[...]).astype(BF16)


def up_terms_kernel(hidden_grad, normed, branch_grad, attended, *refs):
    terms, (up_scratch, out_scratch) = refs[:8], refs[8:]
    emit_terms(normed, hidden_grad, up_scratch, terms, 0)
    emit_terms(attended, branch_grad, out_scratch, terms, hidden_grad.shape[1])


def attend_backward_kernel(
    tiles,
    skipped,
    q_ref,
    own_k,
    own_v,
    other_k,
    other_v,
    qa_ref,
    ka_ref,
    live_ref,
    o_ref,
    lse_ref,
    g_ref,
    dq_ref,
    own_grad_ref,
    other_grad_ref,
    dk_sum,
    dv_sum,
):
    pair = pl.program_id(0) + skipped
    rows = q_ref.shape[0]
    row_tile = rows // tiles
    key_rows = jnp.concatenate([own_k[...], other_k[...]], axis=0)
    keys = jnp.concatenate([key_rows, ka_ref[...]], axis=1)
    values = jnp.concatenate([own_v[...], other_v[...]], axis=0)
    lane = lax.broadcasted_iota(jnp.int32, (row_tile, LANES), 1)
    scale = HEAD_WIDTH**-0.5
    for start in range(0, rows, row_tile):
        here = pl.ds(start, row_tile)
        scaled = q_ref[here, :] * jnp.asarray(scale, BF16)
        marks = qa_ref[here, :]
        grads = (g_ref[here, :] * live_ref[here, :]).astype(BF16)
        both = grads.astype(F32) * o_ref[here, :].astype(F32)
        halves = []
        key_part = value_part = None
        for which in range(2):
            mine = half_lanes(scaled.shape, which)
            own = jnp.where(mine, scaled, jnp.zeros_like(scaled))
            own_grads = jnp.where(mine, grads, jnp.zeros_like(grads))
            row_dot = jnp.sum(jnp.where(mine, both, 0.0), axis=1, keepdims=True)
            lse = jnp.sum(
                jnp.where(lane == 2 * pair + which, lse_ref[here, :], 0.0), axis=1, keepdims=True
            )
            scores = cols_of(jnp.concatenate([own, marks], axis=1), keys)
            probs = jnp.exp(scores - lse)
            prob_grads = cols_of(own_grads, values)
            score_grads = (probs * (prob_grads - row_dot)).astype(BF16)
            halves.append(dot(score_grads, key_rows))
            value_term = rows_of(probs.astype(BF16), own_grads)
            key_term = rows_of(score_grads, own)
            value_part = value_term if which == 0 else value_part + value_term
            key_part = key_term if which == 0 else key_part + key_term
        mixed = jnp.where(lane < HEAD_WIDTH, halves[0], halves[1])
        dq_ref[here, :] = (mixed * scale).astype(BF16)
        if start == 0:
            dk_sum[...] = key_part
            dv_sum[...] = value_part
        else:
            dk_sum[...] += key_part
            dv_sum[...] += value_part
    own_grad_ref[0] = dk_sum[:rows, :].astype(BF16)
    own_grad_ref[1] = dv_sum[:rows, :].astype(BF16)
    other_grad_ref[0] = dk_sum[rows:, :].astype(BF16)
    other_grad_ref[1] = dv_sum[rows:, :].astype(BF16)


def attend_backward(
    first, pairs_here, skipped, q, own_k, own_v, other_k, other_v, q_marks, k_marks, live, attended, lse, grads, after=()
):
    rows = q.shape[0]
    per_pair, _, marks, all_marks = attention_specs(rows, first)
    out_pair, out_two = attention_specs(rows, 0)[:2]
    there = attention_specs(rows, skipped)[0]
    return pl.pallas_call(
        ignoring(partial(attend_backward_kernel, row_tiles(rows), skipped), 11, len(after)),
        grid=(pairs_here,),
        in_specs=[per_pair] * 5 + [marks, all_marks, marks, there, marks, per_pair]
        + [ANY] * len(after),
        out_specs=[out_pair, out_two, out_two],
        out_shape=[shape((rows, pairs_here * LANES))]
        + [shape((2, rows, pairs_here * LANES))] * 2,
        scratch_shapes=[pltpu.VMEM((2 * rows, LANES), F32)] * 2,
        compiler_params=pltpu.CompilerParams(vmem_limit_bytes=(16 if rows <= ROW_TILE else 48) * MIB),
    )(q, own_k, own_v, other_k, other_v, q_marks, k_marks, live, attended, lse, grads, *after)


def emit_terms(left, right, scratch, terms, at):
    mine, core = lax.axis_index("fsdp"), lax.axis_index("seq") % 2
    count, cols = left.shape[1] // 4, right.shape[1]
    half = count // 2
    here = slice(at, at + cols)
    if scratch is not None:
        scratch[...] = rows_of(left[...], right[...])
    for i in range(2):
        home = core ^ i
        for out, flip in zip(terms[4 * i : 4 * i + 4], (3, 2 - home, 1 + home, 0)):
            start = (mine ^ flip) * count + home * half
            if scratch is not None:
                value = scratch[pl.ds(pl.multiple_of(start, 16), half), :]
            else:
                value = rows_of(left[:, pl.ds(pl.multiple_of(start, LANES), half)], right[...])
            out[:, here] = value.astype(BF16)


def term_shapes(rows, cols):
    return [shape((rows // 2, cols))] * 8


class Reduction:
    def __init__(self, terms):
        self.keep_far, self.keep_side, self.keep_near, self.keep_own = terms[:4]
        self.away = terms[4:]
        self.count = self.keep_far.shape[0]

    def send_other(self):
        self.other_far, self.other_side, self.other_near, self.other_own = [
            to_core(item) for item in self.away
        ]
        return [self.other_far, self.other_side, self.other_near, self.other_own]

    def send_far(self):
        self.far = to_fsdp((wide(self.keep_far) + wide(self.other_far)).astype(BF16), (2, 1))
        return [self.far]

    def send_side(self):
        self.side = to_fsdp((wide(self.keep_side) + wide(self.other_side)).astype(BF16), (2, 1))
        return [self.side]

    def send_near(self):
        total = wide(self.keep_near) + wide(self.other_near) + wide(self.far)
        self.near = to_fsdp(total.astype(BF16), (1, 2))
        return [self.near]

    def send_chips(self):
        flips = [1 << i for i in range((lax.axis_size("seq") // 2).bit_length() - 1)]
        self.orders = list(zip(flips, flips[::-1]))
        total = wide(self.keep_own) + wide(self.other_own)
        self.sent = (total + wide(self.near) + wide(self.side)).astype(BF16)
        self.got = to_chip(self.sent, *self.orders[0])
        return [self.got]

    def send_chips_again(self):
        for order in self.orders[1:]:
            self.sent = (wide(self.sent) + wide(self.got)).astype(BF16)
            self.got = to_chip(self.sent, *order)
        return [self.got]

    def send_total(self):
        self.total = (wide(self.sent) + wide(self.got)).astype(BF16)
        self.other_total = to_core(self.total)
        return [self.other_total]

    def shards(self, widths, after=()):
        outs = [shape((2 * self.count, cols), F32) for cols in widths]
        operands = [(self.total, VMEM), (self.other_total, VMEM)]
        return call(spread_kernel, operands, outs, after=after)


def spread_kernel(own_ref, other_ref, *outs):
    core = lax.axis_index("seq") % 2
    half = own_ref.shape[0]
    at = 0
    for out in outs:
        cols = out.shape[1]
        for i, source in enumerate((own_ref, other_ref)):
            start = pl.multiple_of((core ^ i) * half, 16)
            out[pl.ds(start, half), :] = source[:, at : at + cols].astype(F32)
        at += cols


def project_grad_kernel(count, *refs):
    q_grads, own_grads, other_grads = refs[:count], refs[count : 2 * count], refs[2 * count : 3 * count]
    normed, projected_grad, sums = refs[3 * count : 3 * count + 3]
    terms, scratch = refs[3 * count + 3 : 3 * count + 11], refs[3 * count + 11]
    width = normed.shape[1]
    at = 0
    for q_grad, own_grad, other_grad in zip(q_grads, own_grads, other_grads):
        here = slice(at, at + q_grad.shape[1])
        projected_grad[:, here] = q_grad[...]
        sums[0:1, here] = jnp.sum(q_grad[...].astype(F32), axis=0, keepdims=True)
        for i in range(2):
            both = (own_grad[i].astype(F32) + other_grad[i].astype(F32)).astype(BF16)
            first = (i + 1) * width + at
            projected_grad[:, first : first + q_grad.shape[1]] = both
        sums[1:2, here] = jnp.sum(both.astype(F32), axis=0, keepdims=True)
        at += q_grad.shape[1]
    emit_terms(normed, projected_grad, scratch, terms, 0)


def input_kernel(chips, *refs):
    projected_grad, x_rows, middle_grad, vec = refs[:4]
    qkv_sums, narrow_sums, down_shift_grad, scale_grad, up_shift_grad, own = refs[4:10]
    pieces, rest = refs[10:14], refs[14:]
    outs, sums, weight, sems = rest[:chips], rest[chips], rest[chips + 1], rest[chips + 2]
    copies = stage(weight, own, pieces, 0, EXTRA_ROWS, sems)
    capacity, width = outs[0].shape
    wait_all(copies)
    totals = [None] * 2
    for i in range(chips):
        here = slice(i * capacity, (i + 1) * capacity)
        grad = cols_of(projected_grad[here, :], weight[...])
        xhat, rstd = norm_parts(x_rows[here, :].astype(F32))
        back = norm_back(grad * vector(vec, LN1_GAIN), xhat, rstd)
        outs[i][...] = (middle_grad[here, :] + back).astype(BF16)
        for j, term in enumerate((grad * xhat, grad)):
            term = jnp.sum(term, axis=0, keepdims=True)
            totals[j] = term if i == 0 else totals[j] + term
    sums[...] = jnp.zeros_like(sums)
    for row, value in (
        (LN1_GAIN, totals[0]),
        (LN1_BIAS, totals[1]),
        (QUERY_BIAS, qkv_sums[0:1, :]),
        (VALUE_BIAS, qkv_sums[1:2, :]),
        (OUT_BIAS, narrow_sums[3:4, :]),
        (SCALE_ATTN, narrow_sums[2:3, :]),
        (LN2_GAIN, narrow_sums[0:1, :]),
        (LN2_BIAS, narrow_sums[1:2, :]),
        (DOWN_BIAS, down_shift_grad[...]),
        (SCALE_MLP, scale_grad[...]),
    ):
        sums[row : row + 1, :] = value
    for f in range(4):
        sums[UP_ROW + f : UP_ROW + f + 1, :] = up_shift_grad[:, f * width : (f + 1) * width]


def body(
    tokens,
    image_tokens,
    ln1_gain,
    ln1_bias,
    qkv_weight,
    query_bias,
    value_bias,
    out_weight,
    out_bias,
    scale_attn,
    ln2_gain,
    ln2_bias,
    up_weight,
    up_bias,
    down_weight,
    down_bias,
    scale_mlp,
    cotangent,
):
    seq_count = lax.axis_size("seq")
    fsdp_index = lax.axis_index("fsdp")
    chips = seq_count // 2
    micro_count, tok_count, width = tokens.shape[0], tokens.shape[2], tokens.shape[4]
    slots, images = image_tokens.shape[2:]
    assert chips == micro_count * slots and lax.axis_size("fsdp") == 4
    assert slots * images < PAD_SEGMENT
    most_rows = (LONG - 2) // seq_count + 2
    capacity, crossing = ceil_to(most_rows, 16), ceil_to(most_rows, 8)
    rows = chips * capacity
    tile = rows // 2
    hidden_width = up_weight.shape[1]
    sizes = (slots, images, chips, capacity, tok_count, seq_count)
    counts = image_tokens

    def pick(values, limit=16, after=()):
        return list(
            call(
                partial(pick_kernel, sizes),
                [(counts, SMEM), (values.reshape(micro_count * tok_count, width), VMEM)],
                [shape((capacity, width))] * chips,
                after=after,
                limit=limit,
            )
        )

    def line_up(groups, small=(), limit=16, after=()):
        shards = [shard for group in groups for shard in group]
        more = EXTRA_ROWS if small else 0
        outs = [
            shape((group[0].shape[0] + more, sum(shard.shape[1] for shard in group)))
            for group in groups
        ]
        if small:
            outs += [shape(((outs[0].shape[0] + more) // 2, outs[0].shape[1]))]
        return call(
            partial(line_up_kernel, [len(group) for group in groups], len(small)),
            [(item, VMEM) for item in shards + list(small)],
            outs,
            [pltpu.VMEM((EXTRA_ROWS, width), F32)] if small else [],
            after=after,
            limit=limit,
        )

    def cross(parts, bit):
        labels = [label for label in range(chips) if label & bit]
        sent = jnp.concatenate([parts[label][:crossing] for label in labels])
        return to_chip(sent, *flips_of(bit, chips))

    def crossed(parts, moved, bit):
        parts = list(parts)
        for i, label in enumerate(label for label in range(chips) if label & bit):
            piece = moved[i * crossing : (i + 1) * crossing]
            parts[label] = jnp.pad(piece, ((0, capacity - crossing), (0, 0)))
        return parts

    def cross_rest(parts):
        bit = 2
        while 2 * bit < chips:
            parts = crossed(parts, cross(parts, bit), bit)
            bit *= 2
        return parts, cross(parts, bit), bit

    def collect(parts, after=()):
        return call(
            partial(collect_kernel, sizes),
            [(counts, SMEM)] + [(part, VMEM) for part in parts],
            [shape((micro_count * tok_count, width))],
            after=after,
        )[0]

    small = [
        ln1_gain,
        ln1_bias,
        query_bias,
        value_bias,
        out_bias,
        scale_attn,
        ln2_gain,
        ln2_bias,
        down_bias,
        scale_mlp,
    ]
    own_rows = ln1_gain.shape[0]
    qkv_sent, qkv_first = line_up([[qkv_weight]], small + [up_bias], limit=60)
    near, far = to_fsdp(qkv_sent, (1, 2)), to_fsdp(qkv_first, (3, 3))
    x_parts = pick(tokens, limit=60, after=[qkv_sent])
    for label in range(chips - 1, 0, -1):
        x_parts[label] = to_chip(x_parts[label], *flips_of(label, chips))
    cot_sent = pick(cotangent, after=[qkv_sent])
    up_sent, down_sent = line_up([[out_weight, up_weight], [down_weight]], after=[qkv_sent])
    q_marks, k_marks, live = call(
        partial(marks_kernel, sizes),
        [(counts, SMEM)],
        [shape((rows, LANES)), shape((2 * rows, LANES)), shape((rows, LANES), F32)],
        after=[qkv_sent],
    )
    near, far, up_sent = hold([near, far, up_sent], x_parts + [q_marks, down_sent, cot_sent[0]])
    qkv_pieces = [near, to_core(near), far, to_core(far)]
    up_near = to_fsdp(up_sent, (1, 2))

    x_rows, normed_first, q, own_k, own_v, vec, up_shift = call(
        partial(project_kernel, chips),
        [(part, VMEM) for part in x_parts]
        + [(item, ANY) for item in [qkv_sent, qkv_weight] + qkv_pieces],
        [shape((rows, width))] * 5
        + [shape((EXTRA_ROWS, width), F32), shape((1, hidden_width), F32)],
        [
            pltpu.VMEM((width, 3 * width), BF16),
            pltpu.VMEM((4, EXTRA_ROWS, width), BF16),
            STAGE_SEMS,
            pltpu.SemaphoreType.DMA((4,)),
        ],
    )
    down_sent, *cot_sent = hold([down_sent] + cot_sent, [q])
    down_near = to_fsdp(down_sent, (1, 2))
    cot_moved = cross(cot_sent, 1)
    attention = (q, own_k, own_v, to_core(own_k), to_core(own_v), q_marks, k_marks, live)
    spans = [(0, 2), (2, width // LANES - 2)]
    attended_parts, lses = [], []

    def forward(i):
        part, lse = attend_forward(*spans[i], *attention, after=attended_parts[-1:])
        attended_parts.append(part)
        lses.append(lse)
        return part

    up_near, cot_moved = hold([up_near, cot_moved], [forward(0)])
    cot_parts = crossed(cot_sent, cot_moved, 1)
    up_far = to_fsdp(up_near[: own_rows // 2], (2, 1))
    cot_parts, cot_moved, last_bit = cross_rest(cot_parts)
    up_far, down_near, cot_moved = hold([up_far, down_near, cot_moved], [forward(1)])
    cot_parts = crossed(cot_parts, cot_moved, last_bit)
    up_pieces = [up_near, to_core(up_near), up_far, to_core(up_far)]
    down_far = to_fsdp(down_near[: down_weight.shape[0] // 2], (2, 1))
    up_pieces = hold(up_pieces, [])
    (down_near,) = hold([down_near], up_pieces)
    down_other = to_core(down_near)

    up_scratch = [
        pltpu.VMEM((width, width), BF16),
        pltpu.VMEM((width, hidden_width), BF16),
        STAGE_SEMS,
        STAGE_SEMS,
    ]
    attended, branch, middle, normed_second, active, slope = call(
        partial(widen_kernel, len(attended_parts), tile),
        [(item, VMEM) for item in attended_parts + [x_rows, vec, up_shift]]
        + [(item, ANY) for item in [out_weight, up_weight] + up_pieces],
        [
            shape((rows, width)),
            shape((rows, width), F32),
            shape((rows, width), F32),
            shape((rows, width)),
            shape((rows, hidden_width)),
            shape((rows, hidden_width)),
        ],
        up_scratch,
    )
    down_far, down_other = hold([down_far, down_other], [attended])
    far_other = to_core(down_far)
    cot_rows, down_in, down_shift_grad, *down_terms = call(
        partial(down_terms_kernel, chips),
        [(item, VMEM) for item in [active, vec] + cot_parts],
        [shape((rows, width)), shape((rows, width)), shape((1, width), F32)]
        + term_shapes(down_weight.shape[0], width),
        after=[down_far],
    )
    down = Reduction(down_terms)
    down_pieces = [down_near, down_other, down_far, far_other]
    *down.away, down_near, down_other, down_far, far_other = hold(
        list(down.away) + down_pieces, [down_in]
    )
    down_pieces = [down_near, down_other, down_far, far_other]
    others = down.send_other()
    (down.other_far,) = hold(others[:1], [])
    waits = down.send_far() + others[1:]
    results = call(
        partial(down_kernel, chips, tile),
        [(item, VMEM) for item in (active, slope, middle, cot_rows, down_in, vec)]
        + [(item, ANY) for item in [down_weight] + down_pieces],
        [shape((capacity, width))] * chips
        + [
            shape((rows, hidden_width)),
            shape((1, width), F32),
            shape((1, hidden_width), F32),
        ],
        [pltpu.VMEM((hidden_width, width), BF16), STAGE_SEMS],
    )
    out_sent, (hidden_grad, scale_grad, up_shift_grad) = list(results[:chips]), results[chips:]
    down.far, down.other_side, down.other_near, down.other_own = hold(waits, [hidden_grad])
    waits = down.send_near() + down.send_side()
    out_moved = cross(out_sent, 1)

    middle_grad, branch_grad, attended_grad, narrow_sums = call(
        partial(narrow_kernel, tile),
        [(item, VMEM) for item in (hidden_grad, middle, branch, vec)]
        + [(item, ANY) for item in [out_weight, up_weight] + up_pieces]
        + [(cot_rows, VMEM)],
        [
            shape((rows, width), F32),
            shape((rows, width)),
            shape((rows, width)),
            shape((4, width), F32),
        ],
        up_scratch,
    )
    up_terms = call(
        up_terms_kernel,
        [(item, VMEM) for item in (hidden_grad, normed_second, branch_grad, attended)],
        term_shapes(own_rows, hidden_width + width),
        [pltpu.VMEM((width, hidden_width), F32), pltpu.VMEM((width, width), F32)],
    )
    up = Reduction(up_terms)

    query_grads, own_grads, other_grads = [], [], []

    def backward(first, after=()):
        query_grad, own_grad, other_grad = attend_backward(
            first,
            1,
            first - spans[first >= spans[1][0]][0],
            *attention,
            attended_parts[first >= spans[1][0]],
            lses[first >= spans[1][0]],
            attended_grad,
            after=query_grads[-1:] + list(after),
        )
        query_grads.append(query_grad)
        own_grads.append(own_grad)
        other_grads.append(other_grad)
        return query_grad

    def hold_grads(arrays):
        first, count = sent_grads[0], len(arrays)
        items = hold(list(arrays) + other_grads[first:], query_grads[-1:])
        other_grads[first:] = items[count:]
        sent_grads[0] = len(other_grads)
        return items[:count], [to_core(item) for item in other_grads[first:]]

    sent_grads = [0]
    core_grads = []

    down.near, down.side, out_moved, *up.away = hold(
        waits + [out_moved] + list(up.away), up_terms[:1]
    )
    others = up.send_other()
    waits = down.send_chips()
    up.other_far, up.other_side = hold(others[:2], [])
    waits += up.send_far() + up.send_side() + others[2:]
    backward(0)
    backward(1)
    (down.got, up.far, up.side, up.other_near, up.other_own), fresh = hold_grads(waits)
    waits = up.send_near() + down.send_chips_again() + fresh
    backward(2)
    backward(3)
    (up.near, *core_grads), fresh = hold_grads(waits[:1] + waits[2:])
    waits = up.send_chips() + down.send_total() + fresh
    backward(4)
    backward(5)
    (down.other_total, *more), fresh = hold_grads(waits[1:])
    core_grads += more + fresh
    (down_grad,) = down.shards([width])
    out_parts, out_moved, _ = cross_rest(crossed(out_sent, out_moved, 1))

    projected_grad, qkv_sums, *qkv_terms = call(
        partial(project_grad_kernel, len(query_grads)),
        [(item, VMEM) for item in query_grads + own_grads + core_grads + [normed_first]],
        [shape((rows, 3 * width)), shape((2, width), F32)] + term_shapes(own_rows, 3 * width),
        [pltpu.VMEM((width, 3 * width), F32)],
        after=[down_grad],
    )
    qkv = Reduction(qkv_terms)
    *qkv.away, up.got = hold(list(qkv.away) + waits[:1], [projected_grad])
    up_waits = up.send_chips_again()
    others = qkv.send_other()
    qkv.other_far, qkv.other_side = hold(others[:2], [])
    waits = qkv.send_far() + qkv.send_side() + others[2:]
    *in_sent, sums = call(
        partial(input_kernel, chips),
        [(item, VMEM) for item in (projected_grad, x_rows, middle_grad, vec)]
        + [(item, VMEM) for item in (qkv_sums, narrow_sums, down_shift_grad, scale_grad, up_shift_grad)]
        + [(item, ANY) for item in [qkv_weight] + qkv_pieces],
        [shape((capacity, width))] * chips + [shape((EXTRA_ROWS, width), F32)],
        [pltpu.VMEM((width, 3 * width), BF16), STAGE_SEMS],
    )
    qkv.far, qkv.side, qkv.other_near, qkv.other_own, sums, *in_sent = hold(
        waits + [sums] + in_sent, []
    )
    waits = qkv.send_near()
    in_moved = cross(in_sent, 1)
    other_sums = to_core(sums)
    qkv.near, in_moved, up.got, out_moved, sums, other_sums = hold(
        waits + [in_moved] + up_waits + [out_moved, sums, other_sums], []
    )
    out_parts = crossed(out_parts, out_moved, last_bit)
    up.send_total()
    waits = qkv.send_chips()
    in_parts, in_moved, _ = cross_rest(crossed(in_sent, in_moved, 1))
    sums = sums + other_sums
    far_sums = [to_chip(sums, flip) for flip in (1, 2, 3)]
    output = collect(out_parts)
    (up.other_total,) = hold([up.other_total], [output])
    up_grad, out_grad = up.shards([hidden_width, width])
    qkv.got, sums, in_moved, *far_sums = hold(waits + [sums, in_moved] + far_sums, [up_grad])
    waits = qkv.send_chips_again()
    sums = (sums + far_sums[0]) + (far_sums[1] + far_sums[2])
    flip = 4
    while flip < chips:
        sums = sums + to_chip(sums, flip)
        flip *= 2
    far_sums = [to_fsdp(sums, (flip, flip)) for flip in (1, 2, 3)]
    input_grad = collect(crossed(in_parts, in_moved, last_bit))
    qkv.got, sums, *far_sums = hold(waits + [sums] + far_sums, [input_grad])
    sums = (sums + far_sums[0]) + (far_sums[1] + far_sums[2])
    qkv.send_total()
    (qkv_grad,) = qkv.shards([3 * width])
    output, input_grad = output.reshape(tokens.shape), input_grad.reshape(tokens.shape)

    small_grads = lax.dynamic_slice_in_dim(sums[:UP_ROW], fsdp_index * own_rows, own_rows, 1)
    up_shift_total = lax.dynamic_index_in_dim(sums, UP_ROW + fsdp_index, 0, keepdims=False)
    return (
        output,
        input_grad,
        small_grads[LN1_GAIN],
        small_grads[LN1_BIAS],
        qkv_grad,
        small_grads[QUERY_BIAS],
        small_grads[VALUE_BIAS],
        out_grad,
        small_grads[OUT_BIAS],
        small_grads[SCALE_ATTN],
        small_grads[LN2_GAIN],
        small_grads[LN2_BIAS],
        up_grad,
        up_shift_total,
        down_grad,
        small_grads[DOWN_BIAS],
        small_grads[SCALE_MLP],
    )


def solution(mesh):
    vector, matrix = P("fsdp"), P("fsdp", None)
    places = P(None, "fsdp", None, "seq", None)
    return jax.shard_map(
        body,
        mesh=mesh,
        in_specs=(
            places,
            P(None, "fsdp", None, None),
            vector,
            vector,
            matrix,
            vector,
            vector,
            matrix,
            vector,
            vector,
            vector,
            vector,
            matrix,
            vector,
            matrix,
            vector,
            vector,
            places,
        ),
        out_specs=(
            places,
            places,
            vector,
            vector,
            matrix,
            vector,
            vector,
            matrix,
            vector,
            vector,
            vector,
            vector,
            matrix,
            vector,
            matrix,
            vector,
            vector,
        ),
        check_vma=False,
    )
```
